32 devices in a mesh: groups: 2 (over x), own: 16 (over z, y, core).
Axes of the slice: x: 2, y: 2, z: 4, core: 2. Of those that a mesh axis runs over, the one named last changes fastest.
Arguments:
- embeddings: bfloat16 [512, 128, 1280], P(('groups', 'own')), parts along dimension 0, may hold values from -24 to 24
- lengths: int32 [512], P('groups'), parts along dimension 0, may hold values from 1 to 128, 16384 in all
- proj_weight: bfloat16 [1280, 1280], replicated, may hold values from -0.15625 to 0.15625
- slot_of: int32 [512], P('groups'), parts along dimension 0, may hold values from 0 to 255, as said below
- pairs: int32 [768, 2], P(('groups', 'own')), parts along dimension 0, may hold values from 0 to 255, as said below
Outputs:
- interface: float32 [512, 20, 128], P(('groups', 'own')), parts along dimension 0
The draws below stay inside these ranges and needn't reach their ends.
There are 2 independent parts, one for each index of `groups`. The reference program is written for one: setup_inputs(seed, part) draws one part's arguments, and reference() takes and returns one part's arrays. A program takes and returns all parts, laid end to end along the dimension named above; an argument that names none is the same for every part. Nothing has to cross between parts.
Inputs may be any that keep to these rules, and one draw needn't show every extreme that they name: A permutation: protein p is stored in row slot_of[p] of embeddings, on index slot_of[p] // 16 of own. Pair r is held by the owner of its first protein: slot_of[pairs[r, 0]] // 16 == r // 24. The second proteins of one device's 24 pairs are distinct, at most 2 of them stored on any one owner, and every device has some owner that stores exactly 2 of them. A pair may name one protein twice.
All inputs are finite; a program needn't handle non-finite values.
Results may differ from the reference program's by a relative error of at most 0.007.
Values may be sent and summed in bfloat16 or wider, within the bound.
A program may use at most 128 MiB of HBM per device.

```python
import math
import jax
import jax.numpy as jnp
import numpy as np
from jax import lax

D = 1280
HEADS = 20
L = 128
P_DEV = 16
PAIR_DEV = 24
PROTS = 256
PAIRS = 384


def shared_table(key):
    return jax.random.permutation(key, PROTS).astype(jnp.int32)


def draw_slot_of(key, part):
    return shared_table(key)


def draw_pairs(key, part):
    table = shared_table(key)
    protein_of_row = jnp.argsort(table).astype(jnp.int32)
    key = jax.random.fold_in(key, 5)
    owner_count = PROTS // P_DEV
    lowest = max(1, PAIR_DEV - owner_count)
    highest = PAIR_DEV // 2

    def one_device(device_key, device):
        keys = jax.random.split(device_key, 5)
        owner_order = jax.random.permutation(keys[0], owner_count).astype(jnp.int32)
        doubles = jax.random.randint(keys[1], (), lowest, highest + 1)
        position = jnp.arange(PAIR_DEV, dtype=jnp.int32)
        group = jnp.where(position < 2 * doubles, position // 2, position - doubles)
        owner = owner_order[group]
        second_of_two = (position < 2 * doubles) & (position % 2 == 1)
        picks = jax.vmap(lambda small_key: jax.random.permutation(small_key, P_DEV)[:2])(jax.random.split(keys[2], PAIR_DEV))
        chosen = picks[group]
        local = jnp.where(second_of_two, chosen[:, 1], chosen[:, 0]).astype(jnp.int32)
        row_second = owner * P_DEV + local
        row_first = device * P_DEV + jax.random.randint(keys[3], (PAIR_DEV,), 0, P_DEV)
        shuffle = jax.random.permutation(keys[4], PAIR_DEV)
        stacked = jnp.stack([protein_of_row[row_first], protein_of_row[row_second]], axis=1)
        return stacked[shuffle]
    device_keys = jax.random.split(key, owner_count)
    result = jax.vmap(one_device)(device_keys, jnp.arange(owner_count, dtype=jnp.int32))
    return result.reshape(PAIRS, 2).astype(jnp.int32)


def draw_embeddings(key, part):
    key = jax.random.fold_in(key, 7)
    keys = jax.random.split(key, 1)
    values = jax.random.normal(keys[0], (PROTS, L, D), jnp.float32)
    values = jnp.clip(values, -6.0, 6.0)
    return jnp.clip(values, -24.0, 24.0).astype(jnp.bfloat16)


def length_profile(number_of, total, reach, lean):
    portions = [(1 << 20) // math.isqrt(rank ** lean) + 1 for rank in range(2, number_of + 1)]
    spare, counts = total - reach - (number_of - 1), [1] * (number_of - 1)
    while spare > 0:
        free = [i for i in range(number_of - 1) if counts[i] < reach]
        pool, budget = sum([portions[i] for i in free]), spare
        for i in free:
            more = min(reach - counts[i], max(1, budget * portions[i] // pool), spare)
            counts[i] = counts[i] + more
            spare = spare - more
    return np.array([reach] + counts)


def uneven_parts(key, number_of, total, reach, lean):
    if number_of == 2:
        one = jax.random.randint(key, (), max(1, total - reach), min(reach, total - 1) + 1)
        return jnp.stack([one, total - one])
    tallies = jnp.asarray(length_profile(number_of, total, reach, lean), jnp.int32)
    couples = (number_of - 1) // 2
    source_of, receiver = tallies[1:1 + 2 * couples:2], tallies[2:2 + 2 * couples:2]
    margin = jnp.minimum(source_of - 1, reach - receiver)
    moved = jax.random.randint(jax.random.fold_in(key, 1), (couples,), 0, 1 << 20) % (margin + 1)
    tallies = tallies.at[1:1 + 2 * couples:2].set(source_of - moved).at[2:2 + 2 * couples:2].set(receiver + moved)
    return tallies[jax.random.permutation(jax.random.fold_in(key, 2), number_of)]


def gaussian(stream_key, extent, spread, bound, kind=jnp.bfloat16):
    entries = spread * jax.random.normal(stream_key, extent, jnp.float32)
    return jnp.clip(entries, min=-bound, max=bound).astype(kind)


def setup_inputs(seed: int = 0, part: int = 0) -> dict:
    seeds = jax.random.split(jax.random.key(seed), 6)
    part_keys = jax.random.split(jax.random.fold_in(seeds[5], part), 6)
    return {
        "embeddings": draw_embeddings(jax.random.fold_in(jax.random.fold_in(seeds[5], part), 71), part),
        "lengths": uneven_parts(part_keys[1], PROTS, PROTS * L // 2, L, 1).astype(jnp.int32),
        "proj_weight": gaussian(seeds[2], (D, D), D ** -0.5, 0.15625),
        "slot_of": draw_slot_of(jax.random.fold_in(jax.random.fold_in(seeds[5], part), 71), part),
        "pairs": draw_pairs(jax.random.fold_in(jax.random.fold_in(seeds[5], part), 71), part),
    }


def pair_mass(query, partner, len_query, len_partner):
    batch = query.shape[0]
    head_size = D // HEADS
    left = query.astype(jnp.float32).reshape(batch, L, HEADS, head_size)
    right = partner.astype(jnp.float32).reshape(batch, L, HEADS, head_size)
    scores = jnp.einsum('bihe,bjhe->bhij', left, right) / math.sqrt(head_size)
    positions = jnp.arange(L, dtype=jnp.int32)
    rows_live = positions[None, :] < len_query[:, None]
    cols_live = positions[None, :] < len_partner[:, None]
    live = rows_live[:, None, :, None] & cols_live[:, None, None, :]
    masked = jnp.where(live, scores, -1e+30)
    row_top = lax.optimization_barrier(jnp.max(masked, axis=3, keepdims=True))
    row_exp = jnp.where(live, jnp.exp(masked - row_top), 0.0)
    row_total = lax.optimization_barrier(jnp.sum(row_exp, axis=3, keepdims=True)) + jnp.where(rows_live, 0.0, 1.0)[:, None, :, None]
    to_partner = lax.optimization_barrier(jnp.sum(row_exp / row_total, axis=2))
    col_top = lax.optimization_barrier(jnp.max(masked, axis=2, keepdims=True))
    col_exp = jnp.where(live, jnp.exp(masked - col_top), 0.0)
    col_total = lax.optimization_barrier(jnp.sum(col_exp, axis=2, keepdims=True)) + jnp.where(cols_live, 0.0, 1.0)[:, None, None, :]
    to_query = lax.optimization_barrier(jnp.sum(col_exp / col_total, axis=3))
    ratio = len_partner.astype(jnp.float32) / len_query.astype(jnp.float32)
    return (to_query / ratio[:, None, None], to_partner * ratio[:, None, None])

def reference(embeddings, lengths, proj_weight, slot_of, pairs):
    features = jnp.dot(embeddings.reshape(PROTS * L, D), proj_weight, preferred_element_type=jnp.float32)
    features = features.astype(jnp.bfloat16).reshape(PROTS, L, D)
    row_first = jnp.take(slot_of, pairs[:, 0]).astype(jnp.int32)
    row_second = jnp.take(slot_of, pairs[:, 1]).astype(jnp.int32)
    len_first = jnp.take(lengths, pairs[:, 0])
    len_second = jnp.take(lengths, pairs[:, 1])
    blocks = PAIRS // 8
    items = (row_first.reshape(blocks, 8), row_second.reshape(blocks, 8), len_first.reshape(blocks, 8), len_second.reshape(blocks, 8))

    def step(total, item):
        first_rows, second_rows, first_len, second_len = item
        to_first, to_second = pair_mass(jnp.take(features, first_rows, axis=0), jnp.take(features, second_rows, axis=0), first_len, second_len)
        total = total.at[first_rows].add(to_first)
        total = total.at[second_rows].add(to_second)
        return (total, None)
    start = jnp.zeros((PROTS, HEADS, L), jnp.float32)
    result, _ = lax.scan(step, start, items)
    return result
```

```python
import functools
import math

import jax
import jax.numpy as jnp
from jax import lax
from jax.experimental import pallas as pl
from jax.experimental.pallas import tpu as pltpu
from jax.sharding import PartitionSpec as P

HEADS = 20
CAP = 2
HEAD = 64
PLANE = 4
UNROLL = 8
LOW, HIGH = 2.0**-60, 2.0**60
TILE = 256

block_pairs = 8


def pair_mass(query, partner, len_query, len_partner):
    batch, residues, channels = query.shape
    head_size = channels // HEADS
    left = query.reshape(batch, residues, HEADS, head_size)
    right = partner.reshape(batch, residues, HEADS, head_size)
    scores = jnp.einsum(
        "bihe,bjhe->bhij", left, right, preferred_element_type=jnp.float32
    ) / math.sqrt(head_size)
    positions = jnp.arange(residues, dtype=jnp.int32)
    rows_live = positions[None, :] < len_query[:, None]
    cols_live = positions[None, :] < len_partner[:, None]
    live = rows_live[:, None, :, None] & cols_live[:, None, None, :]
    masked = jnp.where(live, scores, -1e30)
    row_top = jnp.max(masked, axis=3, keepdims=True)
    row_exp = jnp.where(live, jnp.exp(masked - row_top), 0.0)
    row_total = (
        jnp.sum(row_exp, axis=3, keepdims=True) + jnp.where(rows_live, 0.0, 1.0)[:, None, :, None]
    )
    to_partner = jnp.sum(row_exp / row_total, axis=2)
    col_top = jnp.max(masked, axis=2, keepdims=True)
    col_exp = jnp.where(live, jnp.exp(masked - col_top), 0.0)
    col_total = (
        jnp.sum(col_exp, axis=2, keepdims=True) + jnp.where(cols_live, 0.0, 1.0)[:, None, None, :]
    )
    to_query = jnp.sum(col_exp / col_total, axis=3)
    ratio = len_partner.astype(jnp.float32) / len_query.astype(jnp.float32)
    return (to_query / ratio[:, None, None], to_partner * ratio[:, None, None])


def local_any(embeddings, lengths, proj_weight, slot_of, pairs):
    per_device, residues, channels = embeddings.shape
    owners = lax.axis_size("own")
    own_index = lax.axis_index("own")
    pair_count = pairs.shape[0]
    row_first = jnp.take(slot_of, pairs[:, 0])
    row_second = jnp.take(slot_of, pairs[:, 1])
    len_first = jnp.take(lengths, pairs[:, 0])
    len_second = jnp.take(lengths, pairs[:, 1])
    local_first = row_first - own_index * per_device
    holder_second = row_second // per_device
    local_second = row_second % per_device
    order_ids = jnp.arange(pair_count, dtype=jnp.int32)
    earlier = (holder_second[:, None] == holder_second[None, :]) & (
        order_ids[None, :] < order_ids[:, None]
    )
    rank = jnp.sum(earlier.astype(jnp.int32), axis=1)
    placed = holder_second * CAP + rank
    slot_count = owners * CAP
    slot_ids = jnp.arange(slot_count, dtype=jnp.int32)
    wanted = (
        jnp.sum(
            jnp.where(placed[:, None] == slot_ids[None, :], local_second[:, None] + 1, 0), axis=0
        )
        - 1
    )
    asked = lax.all_to_all(
        wanted.reshape(owners, CAP), "own", split_axis=0, concat_axis=0, tiled=True
    ).reshape(slot_count)
    features = jnp.dot(
        embeddings.reshape(per_device * residues, channels),
        proj_weight,
        preferred_element_type=jnp.float32,
    )
    features = features.astype(jnp.bfloat16).reshape(per_device, residues, channels)
    outgoing = jnp.take(features, jnp.maximum(asked, 0), axis=0)
    arrived = lax.all_to_all(
        outgoing.reshape(owners, CAP, residues, channels),
        "own",
        split_axis=0,
        concat_axis=0,
        tiled=True,
    )
    arrived = arrived.reshape(slot_count, residues, channels)
    device_rows = jnp.arange(per_device, dtype=jnp.int32)

    def step(carry, item):
        own_total, slot_total = carry
        first_local, slot_place, first_len, second_len = item
        query = jnp.take(features, first_local, axis=0)
        partner = jnp.take(arrived, slot_place, axis=0)
        to_query, to_partner = pair_mass(query, partner, first_len, second_len)
        own_hits = (first_local[:, None] == device_rows[None, :]).astype(jnp.float32)
        slot_hits = (slot_place[:, None] == slot_ids[None, :]).astype(jnp.float32)
        own_total = own_total + jnp.einsum(
            "bp,bhl->phl", own_hits, to_query, precision=lax.Precision.HIGHEST
        )
        slot_total = slot_total + jnp.einsum(
            "bs,bhl->shl", slot_hits, to_partner, precision=lax.Precision.HIGHEST
        )
        return ((own_total, slot_total), None)

    blocks = pair_count // block_pairs
    items = (
        local_first.reshape(blocks, block_pairs),
        placed.reshape(blocks, block_pairs),
        len_first.reshape(blocks, block_pairs),
        len_second.reshape(blocks, block_pairs),
    )
    start = (
        jnp.zeros((per_device, HEADS, residues), jnp.float32),
        jnp.zeros((slot_count, HEADS, residues), jnp.float32),
    )
    (own_total, slot_total), _ = lax.scan(step, start, items)
    slot_rows = slot_ids // CAP * per_device + wanted
    all_rows = jnp.arange(owners * per_device, dtype=jnp.int32)
    row_hits = ((slot_rows[:, None] == all_rows[None, :]) & (wanted >= 0)[:, None]).astype(
        jnp.float32
    )
    spread = jnp.einsum("sr,shl->rhl", row_hits, slot_total, precision=lax.Precision.HIGHEST)
    return own_total + lax.psum_scatter(spread, "own", scatter_dimension=0, tiled=True)


def exchange_kernel(owners, emb_ref, w_ref, main_ref, extra_ref, stage, send_sem, recv_main, recv_extra, fwd_sem, local_sem):
    me = lax.axis_index("own")
    planes = owners // PLANE
    z, part = me // PLANE, me % PLANE
    half = emb_ref.shape[0] // 2
    wide = PLANE * HEAD

    barrier = pltpu.get_barrier_semaphore()
    for k in range(1, owners):
        pl.semaphore_signal(
            barrier, inc=1, device_id={"own": (me + k) % owners}, device_id_type=pl.DeviceIdType.MESH
        )
    pl.semaphore_wait(barrier, owners - 1)

    low = lax.broadcasted_iota(jnp.int32, (TILE, 2 * HEAD), 1) < HEAD

    def project(step, column):
        @pl.loop(0, half // TILE)
        def _(t):
            row = pl.multiple_of(t * TILE, TILE)
            weight = w_ref[:, pl.ds(column, wide)]
            top = jnp.dot(emb_ref[pl.ds(row, TILE), :], weight, preferred_element_type=jnp.float32)
            bottom = jnp.dot(
                emb_ref[pl.ds(half + row, TILE), :], weight, preferred_element_type=jnp.float32
            )
            for g in range(wide // (2 * HEAD)):
                a = top[:, 2 * HEAD * g : 2 * HEAD * (g + 1)]
                b = bottom[:, 2 * HEAD * g : 2 * HEAD * (g + 1)]
                even = jnp.where(low, a, pltpu.roll(b, HEAD, 1))
                odd = jnp.where(low, pltpu.roll(a, HEAD, 1), b)
                stage[step, 2 * g, pl.ds(row, TILE), :] = even.astype(jnp.bfloat16)
                stage[step, 2 * g + 1, pl.ds(row, TILE), :] = odd.astype(jnp.bfloat16)

    def remote(src, dst, send, recv, target):
        return pltpu.make_async_remote_copy(
            src_ref=src,
            dst_ref=dst,
            send_sem=send,
            recv_sem=recv,
            device_id={"own": target},
            device_id_type=pl.DeviceIdType.MESH,
        )

    sent = []
    locals_ = []
    project(0, owners * HEAD)
    for k in (2, 1, 3):
        q = (z + k) % planes
        copy = remote(
            stage.at[0, q], extra_ref.at[me], send_sem.at[0, k], recv_extra.at[me], q * PLANE + part
        )
        copy.start()
        sent.append(copy)
    copy = pltpu.make_async_copy(stage.at[0, z], extra_ref.at[me], local_sem.at[0])
    copy.start()
    locals_.append(copy)
    for j in range(1, PLANE):
        peer = z * PLANE + (part + j) % PLANE
        copy = remote(
            stage.at[0, z], extra_ref.at[me], fwd_sem.at[0, j], recv_extra.at[me], peer
        )
        copy.start()
        sent.append(copy)
    for step, k in enumerate((2, 1, 3, 0), 1):
        plane = (z + k) % planes
        project(step, pl.multiple_of(plane * wide, wide))
        for j in range(PLANE):
            other = (part + j) % PLANE
            if k == 0 and j == 0:
                copy = pltpu.make_async_copy(stage.at[step, other], main_ref.at[me], local_sem.at[1])
                copy.start()
                locals_.append(copy)
                continue
            copy = remote(
                stage.at[step, other],
                main_ref.at[me],
                send_sem.at[step, j],
                recv_main.at[me],
                plane * PLANE + other,
            )
            copy.start()
            sent.append(copy)

    def arrived(ref, sem, source):
        remote(ref.at[source], ref.at[source], fwd_sem.at[0, 0], sem.at[source], (me + 1) % owners).wait_recv()

    for k in (1, 3, 2):
        source = (z + k) % planes * PLANE + part
        arrived(extra_ref, recv_extra, source)
        for j in range(1, PLANE):
            peer = z * PLANE + (part + j) % PLANE
            copy = remote(
                extra_ref.at[source], extra_ref.at[source], fwd_sem.at[k, j], recv_extra.at[source], peer
            )
            copy.start()
            sent.append(copy)
    for k in range(planes):
        for j in range(1, PLANE):
            arrived(extra_ref, recv_extra, (z + k) % planes * PLANE + (part + j) % PLANE)
    for k in range(1, owners):
        arrived(main_ref, recv_main, (me + k) % owners)
    for copy in locals_:
        copy.wait()
    for copy in sent:
        copy.wait_send()


def exchange(owners, emb, weight):
    half = emb.shape[0] // 2
    steps = owners // PLANE + 1
    slab = jax.ShapeDtypeStruct((owners, half, 2 * HEAD), jnp.bfloat16)
    return pl.pallas_call(
        functools.partial(exchange_kernel, owners),
        out_shape=(slab, slab),
        in_specs=[pl.BlockSpec(memory_space=pltpu.VMEM)] * 2,
        out_specs=(pl.BlockSpec(memory_space=pl.ANY),) * 2,
        scratch_shapes=[
            pltpu.VMEM((steps, PLANE, half, 2 * HEAD), jnp.bfloat16),
            pltpu.SemaphoreType.DMA((steps, PLANE)),
            pltpu.SemaphoreType.DMA((owners,)),
            pltpu.SemaphoreType.DMA((owners,)),
            pltpu.SemaphoreType.DMA((owners // PLANE, PLANE)),
            pltpu.SemaphoreType.DMA((2,)),
        ],
        compiler_params=pltpu.CompilerParams(
            collective_id=0, has_side_effects=True, vmem_limit_bytes=40 * 2**20
        ),
        cost_estimate=pl.CostEstimate(
            flops=2 * emb.size * weight.shape[1], bytes_accessed=40 * 2**20, transcendentals=0
        ),
    )(emb, weight)


def pairs_kernel(
    per_device, pair_ref, slot_ref, len_ref, part_ref, main_ref, extra_ref, out_ref, table, row_len
):
    owners, half, lanes = main_ref.shape
    residues = 2 * half // per_device
    prots = slot_ref.shape[0]
    pair_count = pair_ref.shape[0] // 2
    share = pair_count // PLANE
    scale = math.log2(math.e) / math.sqrt(HEAD)

    @pl.loop(0, prots)
    def _(p):
        row_len[slot_ref[p]] = len_ref[p]

    out_ref[...] = jnp.zeros_like(out_ref)
    lane = lax.broadcasted_iota(jnp.int32, (residues, lanes), 1)
    position = lax.broadcasted_iota(jnp.int32, (residues, lanes), 0)
    low = lane < HEAD

    @pl.loop(0, owners)
    def _(source):
        for p in range(per_device // 2):
            m = main_ref[source, p * residues : (p + 1) * residues, :].astype(jnp.float32)
            e = extra_ref[source, p * residues : (p + 1) * residues, :].astype(jnp.float32)
            first = source * per_device + p
            second = first + per_device // 2
            one = jnp.where(low, m, pltpu.roll(e, HEAD, 1))
            two = jnp.where(low, pltpu.roll(m, HEAD, 1), e)
            table[first] = jnp.where(position < row_len[first], one, 0.0).astype(jnp.bfloat16)
            table[second] = jnp.where(position < row_len[second], two, 0.0).astype(jnp.bfloat16)

    small = lax.broadcasted_iota(jnp.int32, (16, lanes), 1)
    top = lax.broadcasted_iota(jnp.int32, (16, lanes), 0) == 0

    def facts(k):
        a, b = pair_ref[2 * k], pair_ref[2 * k + 1]
        return slot_ref[a], slot_ref[b], len_ref[a], len_ref[b]

    def pick(row, extra):
        left = table[row]
        keep = low if not extra else jnp.logical_not(low)
        return jnp.where(keep, left, jnp.zeros_like(left))

    def inner(x, y):
        return lax.dot_general(x, y, (((1,), (1,)), ((), ())), preferred_element_type=jnp.float32)

    def outer(x, y):
        return lax.dot_general(x, y, (((1,), (0,)), ((), ())), preferred_element_type=jnp.float32)

    def two_parts(x):
        high = x.astype(jnp.bfloat16).astype(jnp.float32)
        return jnp.where(top, high, x - high).astype(jnp.bfloat16)

    def ratio_of(number, n_a, n_b):
        fa = jnp.full((1, lanes), n_a, jnp.int32).astype(jnp.float32)
        fb = jnp.full((1, lanes), n_b, jnp.int32).astype(jnp.float32)
        return fa / fb, fb / fa

    def add(row, kind, value):
        owner, place = row // per_device, row % per_device
        out_ref[owner, kind, pl.ds(place, 1), :] += value

    def fast(extra, ks, bad):
        known = [facts(k) for k in ks]
        scores = [inner(pick(ra, extra), table[rb]) for ra, rb, _, _ in known]
        weights = [jnp.exp2(s * scale).astype(jnp.bfloat16) for s in scores]
        live_i = [small < na for _, _, na, _ in known]
        live_j = [small < nb for _, _, _, nb in known]
        row_tot = [
            inner(jnp.where(j, 1.0, 0.0).astype(jnp.bfloat16), w) for j, w in zip(live_j, weights)
        ]
        col_tot = [
            outer(jnp.where(i, 1.0, 0.0).astype(jnp.bfloat16), w) for i, w in zip(live_i, weights)
        ]
        for i, j, r, c in zip(live_i, live_j, row_tot, col_tot):
            fine_r = (r > LOW) & (r < HIGH)
            fine_c = (c > LOW) & (c < HIGH)
            bad = bad + jnp.where(i, jnp.where(fine_r, 0.0, 1.0), 0.0)
            bad = bad + jnp.where(j, jnp.where(fine_c, 0.0, 1.0), 0.0)
        r_inv = [two_parts(jnp.where(i, 1.0 / r, 0.0)) for i, r in zip(live_i, row_tot)]
        c_inv = [two_parts(jnp.where(j, 1.0 / c, 0.0)) for j, c in zip(live_j, col_tot)]
        to_b = [outer(r, w) for r, w in zip(r_inv, weights)]
        to_a = [inner(c, w) for c, w in zip(c_inv, weights)]
        for (ra, rb, na, nb), i, j, a, b in zip(known, live_i, live_j, to_a, to_b):
            a_over_b, b_over_a = ratio_of(None, na, nb)
            add(ra, int(extra), jnp.where(i[:1], (a[0:1] + a[1:2]) * a_over_b, 0.0))
            add(rb, int(extra), jnp.where(j[:1], (b[0:1] + b[1:2]) * b_over_a, 0.0))
        return bad

    def mass(left, right, n_left, n_right):
        live = (position < n_left) & (lane < n_right)
        masked = jnp.where(live, inner(left, right) * scale, -1e30)
        top_row = jnp.max(masked, axis=1, keepdims=True)
        weight = jnp.where(live, jnp.exp2(masked - top_row), 0.0)
        total = jnp.sum(weight, axis=1, keepdims=True)
        total = total + jnp.where(position[:, :1] < n_left, 0.0, 1.0)
        return jnp.sum(weight / total, axis=0, keepdims=True)

    def safe(extra, k):
        ra, rb, na, nb = facts(k)
        left, right = pick(ra, extra), pick(rb, extra)
        a_over_b, b_over_a = ratio_of(None, na, nb)
        add(ra, int(extra), mass(right, left, nb, na) * a_over_b)
        add(rb, int(extra), mass(left, right, na, nb) * b_over_a)

    start = part_ref[0] * share
    bad = jnp.zeros((16, lanes), jnp.float32)
    bad = lax.fori_loop(
        0,
        pair_count // UNROLL,
        lambda t, bad: fast(False, [t * UNROLL + u for u in range(UNROLL)], bad),
        bad,
    )
    bad = lax.fori_loop(
        0,
        share // UNROLL,
        lambda t, bad: fast(True, [start + t * UNROLL + u for u in range(UNROLL)], bad),
        bad,
    )

    @pl.when(jnp.max(bad) > 0.0)
    def _():
        out_ref[...] = jnp.zeros_like(out_ref)

        @pl.loop(0, pair_count)
        def _(k):
            safe(False, k)

        @pl.loop(0, share)
        def _(k):
            safe(True, start + k)


def pair_sums(per_device, pairs, slot_of, lengths, part, main, extra):
    owners, half, lanes = main.shape
    prots = slot_of.shape[0]
    residues = 2 * half // per_device
    smem = pl.BlockSpec(memory_space=pltpu.SMEM)
    vmem = pl.BlockSpec(memory_space=pltpu.VMEM)
    return pl.pallas_call(
        functools.partial(pairs_kernel, per_device),
        out_shape=jax.ShapeDtypeStruct((owners, 2, per_device, residues), jnp.float32),
        in_specs=[smem] * 4 + [vmem] * 2,
        out_specs=vmem,
        scratch_shapes=[
            pltpu.VMEM((prots, residues, lanes), jnp.bfloat16),
            pltpu.SMEM((prots,), jnp.int32),
        ],
        compiler_params=pltpu.CompilerParams(vmem_limit_bytes=44 * 2**20),
    )(pairs, slot_of, lengths, part, main, extra)


def local_split(embeddings, lengths, proj_weight, slot_of, pairs):
    per_device, residues, channels = embeddings.shape
    owners = lax.axis_size("own")
    all_pairs = lax.all_gather(pairs.reshape(-1), "own", tiled=True)
    main, extra = exchange(owners, embeddings.reshape(per_device * residues, channels), proj_weight)
    part = (lax.axis_index("own") % PLANE).reshape(1)
    mass = pair_sums(per_device, all_pairs, slot_of, lengths, part, main, extra)
    back = lax.all_to_all(mass, "own", split_axis=0, concat_axis=0, tiled=True)
    first = back[:, 0]
    rest = back[:, 1].reshape(owners // PLANE, PLANE, per_device, residues).sum(axis=1)
    return jnp.concatenate([first, rest], axis=0).transpose(1, 0, 2)


def split_by_heads(mesh):
    owners = mesh.shape["own"]
    return owners % PLANE == 0 and HEADS == owners + owners // PLANE and owners // PLANE == PLANE


def solution(mesh):
    placed = (
        P(("groups", "own"), None, None),
        P("groups"),
        P(),
        P("groups"),
        P(("groups", "own"), None),
    )
    return jax.shard_map(
        local_split if split_by_heads(mesh) else local_any,
        mesh=mesh,
        in_specs=placed,
        out_specs=P(("groups", "own"), None, None),
        check_vma=False,
    )
```

```python
import functools
import math

import jax
import jax.numpy as jnp
from jax import lax
from jax.experimental import pallas as pl
from jax.experimental.pallas import tpu as pltpu
from jax.sharding import PartitionSpec as P

HEADS = 20
CAP = 2
HEAD = 64
PLANE = 4
UNROLL = 8
LOW, HIGH = 2.0**-60, 2.0**60
GRANULE = 16
LADDER = (22, 23, 24, 26, 32)

block_pairs = 8


def pair_mass(query, partner, len_query, len_partner):
    batch, residues, channels = query.shape
    head_size = channels // HEADS
    left = query.reshape(batch, residues, HEADS, head_size)
    right = partner.reshape(batch, residues, HEADS, head_size)
    scores = jnp.einsum(
        "bihe,bjhe->bhij", left, right, preferred_element_type=jnp.float32
    ) / math.sqrt(head_size)
    positions = jnp.arange(residues, dtype=jnp.int32)
    rows_live = positions[None, :] < len_query[:, None]
    cols_live = positions[None, :] < len_partner[:, None]
    live = rows_live[:, None, :, None] & cols_live[:, None, None, :]
    masked = jnp.where(live, scores, -1e30)
    row_top = jnp.max(masked, axis=3, keepdims=True)
    row_exp = jnp.where(live, jnp.exp(masked - row_top), 0.0)
    row_total = (
        jnp.sum(row_exp, axis=3, keepdims=True) + jnp.where(rows_live, 0.0, 1.0)[:, None, :, None]
    )
    to_partner = jnp.sum(row_exp / row_total, axis=2)
    col_top = jnp.max(masked, axis=2, keepdims=True)
    col_exp = jnp.where(live, jnp.exp(masked - col_top), 0.0)
    col_total = (
        jnp.sum(col_exp, axis=2, keepdims=True) + jnp.where(cols_live, 0.0, 1.0)[:, None, None, :]
    )
    to_query = jnp.sum(col_exp / col_total, axis=3)
    ratio = len_partner.astype(jnp.float32) / len_query.astype(jnp.float32)
    return (to_query / ratio[:, None, None], to_partner * ratio[:, None, None])


def local_any(embeddings, lengths, proj_weight, slot_of, pairs):
    per_device, residues, channels = embeddings.shape
    owners = lax.axis_size("own")
    own_index = lax.axis_index("own")
    pair_count = pairs.shape[0]
    row_first = jnp.take(slot_of, pairs[:, 0])
    row_second = jnp.take(slot_of, pairs[:, 1])
    len_first = jnp.take(lengths, pairs[:, 0])
    len_second = jnp.take(lengths, pairs[:, 1])
    local_first = row_first - own_index * per_device
    holder_second = row_second // per_device
    local_second = row_second % per_device
    order_ids = jnp.arange(pair_count, dtype=jnp.int32)
    earlier = (holder_second[:, None] == holder_second[None, :]) & (
        order_ids[None, :] < order_ids[:, None]
    )
    rank = jnp.sum(earlier.astype(jnp.int32), axis=1)
    placed = holder_second * CAP + rank
    slot_count = owners * CAP
    slot_ids = jnp.arange(slot_count, dtype=jnp.int32)
    wanted = (
        jnp.sum(
            jnp.where(placed[:, None] == slot_ids[None, :], local_second[:, None] + 1, 0), axis=0
        )
        - 1
    )
    asked = lax.all_to_all(
        wanted.reshape(owners, CAP), "own", split_axis=0, concat_axis=0, tiled=True
    ).reshape(slot_count)
    features = jnp.dot(
        embeddings.reshape(per_device * residues, channels),
        proj_weight,
        preferred_element_type=jnp.float32,
    )
    features = features.astype(jnp.bfloat16).reshape(per_device, residues, channels)
    outgoing = jnp.take(features, jnp.maximum(asked, 0), axis=0)
    arrived = lax.all_to_all(
        outgoing.reshape(owners, CAP, residues, channels),
        "own",
        split_axis=0,
        concat_axis=0,
        tiled=True,
    )
    arrived = arrived.reshape(slot_count, residues, channels)
    device_rows = jnp.arange(per_device, dtype=jnp.int32)

    def step(carry, item):
        own_total, slot_total = carry
        first_local, slot_place, first_len, second_len = item
        query = jnp.take(features, first_local, axis=0)
        partner = jnp.take(arrived, slot_place, axis=0)
        to_query, to_partner = pair_mass(query, partner, first_len, second_len)
        own_hits = (first_local[:, None] == device_rows[None, :]).astype(jnp.float32)
        slot_hits = (slot_place[:, None] == slot_ids[None, :]).astype(jnp.float32)
        own_total = own_total + jnp.einsum(
            "bp,bhl->phl", own_hits, to_query, precision=lax.Precision.HIGHEST
        )
        slot_total = slot_total + jnp.einsum(
            "bs,bhl->shl", slot_hits, to_partner, precision=lax.Precision.HIGHEST
        )
        return ((own_total, slot_total), None)

    blocks = pair_count // block_pairs
    items = (
        local_first.reshape(blocks, block_pairs),
        placed.reshape(blocks, block_pairs),
        len_first.reshape(blocks, block_pairs),
        len_second.reshape(blocks, block_pairs),
    )
    start = (
        jnp.zeros((per_device, HEADS, residues), jnp.float32),
        jnp.zeros((slot_count, HEADS, residues), jnp.float32),
    )
    (own_total, slot_total), _ = lax.scan(step, start, items)
    slot_rows = slot_ids // CAP * per_device + wanted
    all_rows = jnp.arange(owners * per_device, dtype=jnp.int32)
    row_hits = ((slot_rows[:, None] == all_rows[None, :]) & (wanted >= 0)[:, None]).astype(
        jnp.float32
    )
    spread = jnp.einsum("sr,shl->rhl", row_hits, slot_total, precision=lax.Precision.HIGHEST)
    return own_total + lax.psum_scatter(spread, "own", scatter_dimension=0, tiled=True)


def exchange_kernel(
    owners, packed, w_ref, main_ref, extra_ref, stage, send_sem, recv_main, recv_extra, fwd_sem, local_sem
):
    me = lax.axis_index("own")
    planes = owners // PLANE
    z, part = me // PLANE, me % PLANE
    half = packed.shape[0] // 2
    tile = half // 2
    wide = PLANE * HEAD

    barrier = pltpu.get_barrier_semaphore()
    for k in range(1, owners):
        pl.semaphore_signal(
            barrier, inc=1, device_id={"own": (me + k) % owners}, device_id_type=pl.DeviceIdType.MESH
        )
    pl.semaphore_wait(barrier, owners - 1)

    low = lax.broadcasted_iota(jnp.int32, (tile, 2 * HEAD), 1) < HEAD

    def project(step, column):
        @pl.loop(0, half // tile)
        def _(t):
            row = pl.multiple_of(t * tile, tile)
            weight = w_ref[:, pl.ds(column, wide)]
            top = jnp.dot(packed[pl.ds(row, tile), :], weight, preferred_element_type=jnp.float32)
            bottom = jnp.dot(
                packed[pl.ds(half + row, tile), :], weight, preferred_element_type=jnp.float32
            )
            for g in range(wide // (2 * HEAD)):
                a = top[:, 2 * HEAD * g : 2 * HEAD * (g + 1)]
                b = bottom[:, 2 * HEAD * g : 2 * HEAD * (g + 1)]
                even = jnp.where(low, a, pltpu.roll(b, HEAD, 1))
                odd = jnp.where(low, pltpu.roll(a, HEAD, 1), b)
                stage[step, 2 * g, pl.ds(row, tile), :] = even.astype(jnp.bfloat16)
                stage[step, 2 * g + 1, pl.ds(row, tile), :] = odd.astype(jnp.bfloat16)

    def remote(src, dst, send, recv, target):
        return pltpu.make_async_remote_copy(
            src_ref=src,
            dst_ref=dst,
            send_sem=send,
            recv_sem=recv,
            device_id={"own": target},
            device_id_type=pl.DeviceIdType.MESH,
        )

    sent = []
    locals_ = []
    project(0, owners * HEAD)
    for k in (2, 1, 3):
        q = (z + k) % planes
        copy = remote(
            stage.at[0, q], extra_ref.at[me], send_sem.at[0, k], recv_extra.at[me], q * PLANE + part
        )
        copy.start()
        sent.append(copy)
    copy = pltpu.make_async_copy(stage.at[0, z], extra_ref.at[me], local_sem.at[0])
    copy.start()
    locals_.append(copy)
    for j in range(1, PLANE):
        peer = z * PLANE + (part + j) % PLANE
        copy = remote(
            stage.at[0, z], extra_ref.at[me], fwd_sem.at[0, j], recv_extra.at[me], peer
        )
        copy.start()
        sent.append(copy)
    for step, k in enumerate((2, 1, 3, 0), 1):
        plane = (z + k) % planes
        project(step, pl.multiple_of(plane * wide, wide))
        for j in range(PLANE):
            other = (part + j) % PLANE
            if k == 0 and j == 0:
                copy = pltpu.make_async_copy(stage.at[step, other], main_ref.at[me], local_sem.at[1])
                copy.start()
                locals_.append(copy)
                continue
            copy = remote(
                stage.at[step, other],
                main_ref.at[me],
                send_sem.at[step, j],
                recv_main.at[me],
                plane * PLANE + other,
            )
            copy.start()
            sent.append(copy)

    def arrived(ref, sem, source):
        remote(ref.at[source], ref.at[source], fwd_sem.at[0, 0], sem.at[source], (me + 1) % owners).wait_recv()

    for k in (1, 3, 2):
        source = (z + k) % planes * PLANE + part
        arrived(extra_ref, recv_extra, source)
        for j in range(1, PLANE):
            peer = z * PLANE + (part + j) % PLANE
            copy = remote(
                extra_ref.at[source], extra_ref.at[source], fwd_sem.at[k, j], recv_extra.at[source], peer
            )
            copy.start()
            sent.append(copy)
    for k in range(planes):
        for j in range(1, PLANE):
            arrived(extra_ref, recv_extra, (z + k) % planes * PLANE + (part + j) % PLANE)
    for k in range(1, owners):
        arrived(main_ref, recv_main, (me + k) % owners)
    for copy in locals_:
        copy.wait()
    for copy in sent:
        copy.wait_send()


def pack_kernel(source_ref, emb_ref, packed):
    @pl.loop(0, packed.shape[0] // GRANULE, unroll=4)
    def _(g):
        start = pl.multiple_of(source_ref[g] * GRANULE, GRANULE)
        here = pl.multiple_of(g * GRANULE, GRANULE)
        packed[pl.ds(here, GRANULE), :] = emb_ref[pl.ds(start, GRANULE), :]


def pack(half, source, emb):
    return pl.pallas_call(
        pack_kernel,
        out_shape=jax.ShapeDtypeStruct((2 * half, emb.shape[1]), jnp.bfloat16),
        in_specs=[
            pl.BlockSpec(memory_space=pltpu.SMEM),
            pl.BlockSpec(memory_space=pltpu.VMEM),
        ],
        out_specs=pl.BlockSpec(memory_space=pltpu.VMEM),
        compiler_params=pltpu.CompilerParams(vmem_limit_bytes=20 * 2**20),
    )(source, emb)


def exchange(owners, half, kernel_id, emb, weight):
    steps = owners // PLANE + 1
    slab = jax.ShapeDtypeStruct((owners, half, 2 * HEAD), jnp.bfloat16)
    return pl.pallas_call(
        functools.partial(exchange_kernel, owners),
        out_shape=(slab, slab),
        in_specs=[pl.BlockSpec(memory_space=pltpu.VMEM)] * 2,
        out_specs=(pl.BlockSpec(memory_space=pl.ANY),) * 2,
        scratch_shapes=[
            pltpu.VMEM((steps, PLANE, half, 2 * HEAD), jnp.bfloat16),
            pltpu.SemaphoreType.DMA((steps, PLANE)),
            pltpu.SemaphoreType.DMA((owners,)),
            pltpu.SemaphoreType.DMA((owners,)),
            pltpu.SemaphoreType.DMA((owners // PLANE, PLANE)),
            pltpu.SemaphoreType.DMA((2,)),
        ],
        compiler_params=pltpu.CompilerParams(
            collective_id=kernel_id, has_side_effects=True, vmem_limit_bytes=40 * 2**20
        ),
        cost_estimate=pl.CostEstimate(
            flops=4 * half * weight.size, bytes_accessed=40 * 2**20, transcendentals=0
        ),
    )(emb, weight)


def pairs_kernel(
    per_device, pair_ref, slot_ref, len_ref, start_ref, part_ref, main_ref, extra_ref, out_ref, table
):
    owners, half, lanes = main_ref.shape
    residues = out_ref.shape[3]
    pair_count = pair_ref.shape[0] // 2
    share = pair_count // PLANE
    scale = math.log2(math.e) / math.sqrt(HEAD)

    out_ref[...] = jnp.zeros_like(out_ref)
    lane = lax.broadcasted_iota(jnp.int32, (residues, lanes), 1)
    position = lax.broadcasted_iota(jnp.int32, (residues, lanes), 0)
    low = lane < HEAD

    table[owners * 2 * half :, :] = jnp.zeros((residues, lanes), jnp.bfloat16)
    strip = half // 2
    low_strip = lax.broadcasted_iota(jnp.int32, (strip, lanes), 1) < HEAD

    @pl.loop(0, owners)
    def _(source):
        for p in range(half // strip):
            m = main_ref[source, p * strip : (p + 1) * strip, :].astype(jnp.float32)
            e = extra_ref[source, p * strip : (p + 1) * strip, :].astype(jnp.float32)
            first = pl.multiple_of(source * 2 * half + p * strip, GRANULE)
            second = pl.multiple_of(source * 2 * half + half + p * strip, GRANULE)
            one = jnp.where(low_strip, m, pltpu.roll(e, HEAD, 1))
            two = jnp.where(low_strip, pltpu.roll(m, HEAD, 1), e)
            table[pl.ds(first, strip), :] = one.astype(jnp.bfloat16)
            table[pl.ds(second, strip), :] = two.astype(jnp.bfloat16)

    small = lax.broadcasted_iota(jnp.int32, (16, lanes), 1)
    top = lax.broadcasted_iota(jnp.int32, (16, lanes), 0) == 0

    def facts(k):
        a, b = pair_ref[2 * k], pair_ref[2 * k + 1]
        return slot_ref[a], slot_ref[b], len_ref[a], len_ref[b]

    def rows(row):
        start = row // per_device * (2 * half) + start_ref[row] * GRANULE
        return table[pl.ds(pl.multiple_of(start, GRANULE), residues), :]

    def pick(row, extra):
        left = rows(row)
        keep = low if not extra else jnp.logical_not(low)
        return jnp.where(keep, left, jnp.zeros_like(left))

    def inner(x, y):
        return lax.dot_general(x, y, (((1,), (1,)), ((), ())), preferred_element_type=jnp.float32)

    def outer(x, y):
        return lax.dot_general(x, y, (((1,), (0,)), ((), ())), preferred_element_type=jnp.float32)

    def two_parts(x):
        high = x.astype(jnp.bfloat16).astype(jnp.float32)
        return jnp.where(top, high, x - high).astype(jnp.bfloat16)

    def ratio_of(number, n_a, n_b):
        fa = jnp.full((1, lanes), n_a, jnp.int32).astype(jnp.float32)
        fb = jnp.full((1, lanes), n_b, jnp.int32).astype(jnp.float32)
        return fa / fb, fb / fa

    def add(row, kind, value):
        owner, place = row // per_device, row % per_device
        out_ref[owner, kind, pl.ds(place, 1), :] += value

    def fast(extra, ks, bad):
        known = [facts(k) for k in ks]
        scores = [inner(pick(ra, extra), rows(rb)) for ra, rb, _, _ in known]
        weights = [jnp.exp2(s * scale).astype(jnp.bfloat16) for s in scores]
        live_i = [small < na for _, _, na, _ in known]
        live_j = [small < nb for _, _, _, nb in known]
        row_tot = [
            inner(jnp.where(j, 1.0, 0.0).astype(jnp.bfloat16), w) for j, w in zip(live_j, weights)
        ]
        col_tot = [
            outer(jnp.where(i, 1.0, 0.0).astype(jnp.bfloat16), w) for i, w in zip(live_i, weights)
        ]
        for i, j, r, c in zip(live_i, live_j, row_tot, col_tot):
            fine_r = (r > LOW) & (r < HIGH)
            fine_c = (c > LOW) & (c < HIGH)
            bad = bad + jnp.where(i, jnp.where(fine_r, 0.0, 1.0), 0.0)
            bad = bad + jnp.where(j, jnp.where(fine_c, 0.0, 1.0), 0.0)
        r_inv = [two_parts(jnp.where(i, 1.0 / r, 0.0)) for i, r in zip(live_i, row_tot)]
        c_inv = [two_parts(jnp.where(j, 1.0 / c, 0.0)) for j, c in zip(live_j, col_tot)]
        to_b = [outer(r, w) for r, w in zip(r_inv, weights)]
        to_a = [inner(c, w) for c, w in zip(c_inv, weights)]
        for (ra, rb, na, nb), i, j, a, b in zip(known, live_i, live_j, to_a, to_b):
            a_over_b, b_over_a = ratio_of(None, na, nb)
            add(ra, int(extra), jnp.where(i[:1], (a[0:1] + a[1:2]) * a_over_b, 0.0))
            add(rb, int(extra), jnp.where(j[:1], (b[0:1] + b[1:2]) * b_over_a, 0.0))
        return bad

    def mass(left, right, n_left, n_right):
        live = (position < n_left) & (lane < n_right)
        masked = jnp.where(live, inner(left, right) * scale, -1e30)
        top_row = jnp.max(masked, axis=1, keepdims=True)
        weight = jnp.where(live, jnp.exp2(masked - top_row), 0.0)
        total = jnp.sum(weight, axis=1, keepdims=True)
        total = total + jnp.where(position[:, :1] < n_left, 0.0, 1.0)
        return jnp.sum(weight / total, axis=0, keepdims=True)

    def safe(extra, k):
        ra, rb, na, nb = facts(k)
        left, right = pick(ra, extra), pick(rb, extra)
        a_over_b, b_over_a = ratio_of(None, na, nb)
        add(ra, int(extra), mass(right, left, nb, na) * a_over_b)
        add(rb, int(extra), mass(left, right, na, nb) * b_over_a)

    start = part_ref[0] * share
    bad = jnp.zeros((16, lanes), jnp.float32)
    bad = lax.fori_loop(
        0,
        pair_count // UNROLL,
        lambda t, bad: fast(False, [t * UNROLL + u for u in range(UNROLL)], bad),
        bad,
    )
    bad = lax.fori_loop(
        0,
        share // UNROLL,
        lambda t, bad: fast(True, [start + t * UNROLL + u for u in range(UNROLL)], bad),
        bad,
    )

    @pl.when(jnp.max(bad) > 0.0)
    def _():
        out_ref[...] = jnp.zeros_like(out_ref)

        @pl.loop(0, pair_count)
        def _(k):
            safe(False, k)

        @pl.loop(0, share)
        def _(k):
            safe(True, start + k)


def pair_sums(per_device, residues, pairs, slot_of, lengths, starts, part, main, extra):
    owners, half, lanes = main.shape
    smem = pl.BlockSpec(memory_space=pltpu.SMEM)
    vmem = pl.BlockSpec(memory_space=pltpu.VMEM)
    return pl.pallas_call(
        functools.partial(pairs_kernel, per_device),
        out_shape=jax.ShapeDtypeStruct((owners, 2, per_device, residues), jnp.float32),
        in_specs=[smem] * 5 + [vmem] * 2,
        out_specs=vmem,
        scratch_shapes=[
            pltpu.VMEM((owners * 2 * half + residues, lanes), jnp.bfloat16),
        ],
        compiler_params=pltpu.CompilerParams(vmem_limit_bytes=44 * 2**20),
    )(pairs, slot_of, lengths, starts, part, main, extra)


def local_split(embeddings, lengths, proj_weight, slot_of, pairs):
    per_device, residues, channels = embeddings.shape
    owners = lax.axis_size("own")
    own = lax.axis_index("own")
    full = per_device * residues // 2
    ladder = [full * step // LADDER[-1] for step in LADDER]
    row_ids = jnp.arange(owners * per_device, dtype=jnp.int32)
    row_len = jnp.sum(jnp.where(slot_of[None, :] == row_ids[:, None], lengths[None, :], 0), axis=1)
    count = ((row_len + GRANULE - 1) // GRANULE).reshape(owners, per_device)
    place = jnp.arange(per_device, dtype=jnp.int32)
    starts = jnp.sum(jnp.where(place[None, None, :] < place[None, :, None], count[:, None, :], 0), axis=2)
    need = jnp.max(jnp.sum(count, axis=1))
    sent = jnp.concatenate([pairs.reshape(-1), need.reshape(1)])
    known = lax.all_gather(sent, ("groups", "own"))
    known = known.reshape(lax.axis_size("groups"), owners, -1)
    need = jnp.max(known[:, :, -1])
    all_pairs = lax.dynamic_index_in_dim(known, lax.axis_index("groups"), 0, False)[:, :-1].reshape(-1)
    my_start = lax.dynamic_index_in_dim(starts, own, 0, False)
    my_count = lax.dynamic_index_in_dim(count, own, 0, False)
    granules = jnp.arange(2 * full // GRANULE, dtype=jnp.int32)
    offset = granules[:, None] - my_start[None, :]
    source = jnp.sum(
        jnp.where(
            (offset >= 0) & (offset < my_count[None, :]),
            offset + place[None, :] * (residues // GRANULE),
            0,
        ),
        axis=1,
    )
    part = (own % PLANE).reshape(1)
    rows = embeddings.reshape(per_device * residues, channels)

    def branch(kernel_id, half):
        def run():
            main, extra = exchange(owners, half, kernel_id, pack(half, source, rows), proj_weight)
            return pair_sums(
                per_device, residues, all_pairs, slot_of, lengths, starts.reshape(-1), part, main, extra
            )

        return run

    choice = sum((need * GRANULE > 2 * half).astype(jnp.int32) for half in ladder[:-1])
    mass = lax.switch(choice, [branch(k, half) for k, half in enumerate(ladder)])
    back = lax.all_to_all(mass, "own", split_axis=0, concat_axis=0, tiled=True)
    first = back[:, 0]
    rest = back[:, 1].reshape(owners // PLANE, PLANE, per_device, residues).sum(axis=1)
    return jnp.concatenate([first, rest], axis=0).transpose(1, 0, 2)


def split_by_heads(mesh):
    owners = mesh.shape["own"]
    return owners % PLANE == 0 and HEADS == owners + owners // PLANE and owners // PLANE == PLANE


def solution(mesh):
    placed = (
        P(("groups", "own"), None, None),
        P("groups"),
        P(),
        P("groups"),
        P(("groups", "own"), None),
    )
    return jax.shard_map(
        local_split if split_by_heads(mesh) else local_any,
        mesh=mesh,
        in_specs=placed,
        out_specs=P(("groups", "own"), None, None),
        check_vma=False,
    )
```

```python
import functools
import math

import jax
import jax.numpy as jnp
from jax import lax
from jax.experimental import pallas as pl
from jax.experimental.pallas import tpu as pltpu
from jax.sharding import PartitionSpec as P

HEADS = 20
CAP = 2
HEAD = 64
PLANE = 4
UNROLL = 8
LOW, HIGH = 2.0**-60, 2.0**60
GRANULE = 16
LADDER = (22, 23, 24, 26, 32)

block_pairs = 8


def pair_mass(query, partner, len_query, len_partner):
    batch, residues, channels = query.shape
    head_size = channels // HEADS
    left = query.reshape(batch, residues, HEADS, head_size)
    right = partner.reshape(batch, residues, HEADS, head_size)
    scores = jnp.einsum(
        "bihe,bjhe->bhij", left, right, preferred_element_type=jnp.float32
    ) / math.sqrt(head_size)
    positions = jnp.arange(residues, dtype=jnp.int32)
    rows_live = positions[None, :] < len_query[:, None]
    cols_live = positions[None, :] < len_partner[:, None]
    live = rows_live[:, None, :, None] & cols_live[:, None, None, :]
    masked = jnp.where(live, scores, -1e30)
    row_top = jnp.max(masked, axis=3, keepdims=True)
    row_exp = jnp.where(live, jnp.exp(masked - row_top), 0.0)
    row_total = (
        jnp.sum(row_exp, axis=3, keepdims=True) + jnp.where(rows_live, 0.0, 1.0)[:, None, :, None]
    )
    to_partner = jnp.sum(row_exp / row_total, axis=2)
    col_top = jnp.max(masked, axis=2, keepdims=True)
    col_exp = jnp.where(live, jnp.exp(masked - col_top), 0.0)
    col_total = (
        jnp.sum(col_exp, axis=2, keepdims=True) + jnp.where(cols_live, 0.0, 1.0)[:, None, None, :]
    )
    to_query = jnp.sum(col_exp / col_total, axis=3)
    ratio = len_partner.astype(jnp.float32) / len_query.astype(jnp.float32)
    return (to_query / ratio[:, None, None], to_partner * ratio[:, None, None])


def local_any(embeddings, lengths, proj_weight, slot_of, pairs):
    per_device, residues, channels = embeddings.shape
    owners = lax.axis_size("own")
    own_index = lax.axis_index("own")
    pair_count = pairs.shape[0]
    row_first = jnp.take(slot_of, pairs[:, 0])
    row_second = jnp.take(slot_of, pairs[:, 1])
    len_first = jnp.take(lengths, pairs[:, 0])
    len_second = jnp.take(lengths, pairs[:, 1])
    local_first = row_first - own_index * per_device
    holder_second = row_second // per_device
    local_second = row_second % per_device
    order_ids = jnp.arange(pair_count, dtype=jnp.int32)
    earlier = (holder_second[:, None] == holder_second[None, :]) & (
        order_ids[None, :] < order_ids[:, None]
    )
    rank = jnp.sum(earlier.astype(jnp.int32), axis=1)
    placed = holder_second * CAP + rank
    slot_count = owners * CAP
    slot_ids = jnp.arange(slot_count, dtype=jnp.int32)
    wanted = (
        jnp.sum(
            jnp.where(placed[:, None] == slot_ids[None, :], local_second[:, None] + 1, 0), axis=0
        )
        - 1
    )
    asked = lax.all_to_all(
        wanted.reshape(owners, CAP), "own", split_axis=0, concat_axis=0, tiled=True
    ).reshape(slot_count)
    features = jnp.dot(
        embeddings.reshape(per_device * residues, channels),
        proj_weight,
        preferred_element_type=jnp.float32,
    )
    features = features.astype(jnp.bfloat16).reshape(per_device, residues, channels)
    outgoing = jnp.take(features, jnp.maximum(asked, 0), axis=0)
    arrived = lax.all_to_all(
        outgoing.reshape(owners, CAP, residues, channels),
        "own",
        split_axis=0,
        concat_axis=0,
        tiled=True,
    )
    arrived = arrived.reshape(slot_count, residues, channels)
    device_rows = jnp.arange(per_device, dtype=jnp.int32)

    def step(carry, item):
        own_total, slot_total = carry
        first_local, slot_place, first_len, second_len = item
        query = jnp.take(features, first_local, axis=0)
        partner = jnp.take(arrived, slot_place, axis=0)
        to_query, to_partner = pair_mass(query, partner, first_len, second_len)
        own_hits = (first_local[:, None] == device_rows[None, :]).astype(jnp.float32)
        slot_hits = (slot_place[:, None] == slot_ids[None, :]).astype(jnp.float32)
        own_total = own_total + jnp.einsum(
            "bp,bhl->phl", own_hits, to_query, precision=lax.Precision.HIGHEST
        )
        slot_total = slot_total + jnp.einsum(
            "bs,bhl->shl", slot_hits, to_partner, precision=lax.Precision.HIGHEST
        )
        return ((own_total, slot_total), None)

    blocks = pair_count // block_pairs
    items = (
        local_first.reshape(blocks, block_pairs),
        placed.reshape(blocks, block_pairs),
        len_first.reshape(blocks, block_pairs),
        len_second.reshape(blocks, block_pairs),
    )
    start = (
        jnp.zeros((per_device, HEADS, residues), jnp.float32),
        jnp.zeros((slot_count, HEADS, residues), jnp.float32),
    )
    (own_total, slot_total), _ = lax.scan(step, start, items)
    slot_rows = slot_ids // CAP * per_device + wanted
    all_rows = jnp.arange(owners * per_device, dtype=jnp.int32)
    row_hits = ((slot_rows[:, None] == all_rows[None, :]) & (wanted >= 0)[:, None]).astype(
        jnp.float32
    )
    spread = jnp.einsum("sr,shl->rhl", row_hits, slot_total, precision=lax.Precision.HIGHEST)
    return own_total + lax.psum_scatter(spread, "own", scatter_dimension=0, tiled=True)


def exchange_kernel(
    owners,
    pair_ref,
    packed,
    w_ref,
    known_ref,
    main_ref,
    extra_ref,
    stage,
    send_sem,
    recv_main,
    recv_extra,
    fwd_sem,
    local_sem,
    pair_sem,
    recv_pair,
):
    me = lax.axis_index("own")
    planes = owners // PLANE
    z, part = me // PLANE, me % PLANE
    half = packed.shape[0] // 2
    tile = half // 2
    wide = PLANE * HEAD

    barrier = pltpu.get_barrier_semaphore()
    for k in range(1, owners):
        pl.semaphore_signal(
            barrier, inc=1, device_id={"own": (me + k) % owners}, device_id_type=pl.DeviceIdType.MESH
        )
    pl.semaphore_wait(barrier, owners - 1)

    low = lax.broadcasted_iota(jnp.int32, (tile, 2 * HEAD), 1) < HEAD

    def project(step, column):
        @pl.loop(0, half // tile)
        def _(t):
            row = pl.multiple_of(t * tile, tile)
            weight = w_ref[:, pl.ds(column, wide)]
            top = jnp.dot(packed[pl.ds(row, tile), :], weight, preferred_element_type=jnp.float32)
            bottom = jnp.dot(
                packed[pl.ds(half + row, tile), :], weight, preferred_element_type=jnp.float32
            )
            for g in range(wide // (2 * HEAD)):
                a = top[:, 2 * HEAD * g : 2 * HEAD * (g + 1)]
                b = bottom[:, 2 * HEAD * g : 2 * HEAD * (g + 1)]
                even = jnp.where(low, a, pltpu.roll(b, HEAD, 1))
                odd = jnp.where(low, pltpu.roll(a, HEAD, 1), b)
                stage[step, 2 * g, pl.ds(row, tile), :] = even.astype(jnp.bfloat16)
                stage[step, 2 * g + 1, pl.ds(row, tile), :] = odd.astype(jnp.bfloat16)

    def remote(src, dst, send, recv, target):
        return pltpu.make_async_remote_copy(
            src_ref=src,
            dst_ref=dst,
            send_sem=send,
            recv_sem=recv,
            device_id={"own": target},
            device_id_type=pl.DeviceIdType.MESH,
        )

    sent = []
    locals_ = []
    for k in range(1, owners):
        copy = remote(
            pair_ref, known_ref.at[me], pair_sem.at[k], recv_pair.at[me], (me + k) % owners
        )
        copy.start()
        sent.append(copy)
    copy = pltpu.make_async_copy(pair_ref, known_ref.at[me], local_sem.at[2])
    copy.start()
    locals_.append(copy)
    project(0, owners * HEAD)
    for k in (2, 1, 3):
        q = (z + k) % planes
        copy = remote(
            stage.at[0, q], extra_ref.at[me], send_sem.at[0, k], recv_extra.at[me], q * PLANE + part
        )
        copy.start()
        sent.append(copy)
    copy = pltpu.make_async_copy(stage.at[0, z], extra_ref.at[me], local_sem.at[0])
    copy.start()
    locals_.append(copy)
    for j in range(1, PLANE):
        peer = z * PLANE + (part + j) % PLANE
        copy = remote(
            stage.at[0, z], extra_ref.at[me], fwd_sem.at[0, j], recv_extra.at[me], peer
        )
        copy.start()
        sent.append(copy)
    for step, k in enumerate((2, 1, 3, 0), 1):
        plane = (z + k) % planes
        project(step, pl.multiple_of(plane * wide, wide))
        for j in range(PLANE):
            other = (part + j) % PLANE
            if k == 0 and j == 0:
                copy = pltpu.make_async_copy(stage.at[step, other], main_ref.at[me], local_sem.at[1])
                copy.start()
                locals_.append(copy)
                continue
            copy = remote(
                stage.at[step, other],
                main_ref.at[me],
                send_sem.at[step, j],
                recv_main.at[me],
                plane * PLANE + other,
            )
            copy.start()
            sent.append(copy)

    def arrived(ref, sem, source):
        remote(ref.at[source], ref.at[source], fwd_sem.at[0, 0], sem.at[source], (me + 1) % owners).wait_recv()

    for k in (1, 3, 2):
        source = (z + k) % planes * PLANE + part
        arrived(extra_ref, recv_extra, source)
        for j in range(1, PLANE):
            peer = z * PLANE + (part + j) % PLANE
            copy = remote(
                extra_ref.at[source], extra_ref.at[source], fwd_sem.at[k, j], recv_extra.at[source], peer
            )
            copy.start()
            sent.append(copy)
    for k in range(planes):
        for j in range(1, PLANE):
            arrived(extra_ref, recv_extra, (z + k) % planes * PLANE + (part + j) % PLANE)
    for k in range(1, owners):
        arrived(known_ref, recv_pair, (me + k) % owners)
        arrived(main_ref, recv_main, (me + k) % owners)
    for copy in locals_:
        copy.wait()
    for copy in sent:
        copy.wait_send()


def pack_kernel(source_ref, emb_ref, packed):
    @pl.loop(0, packed.shape[0] // GRANULE, unroll=4)
    def _(g):
        start = pl.multiple_of(source_ref[g] * GRANULE, GRANULE)
        here = pl.multiple_of(g * GRANULE, GRANULE)
        packed[pl.ds(here, GRANULE), :] = emb_ref[pl.ds(start, GRANULE), :]


def pack(half, source, emb):
    return pl.pallas_call(
        pack_kernel,
        out_shape=jax.ShapeDtypeStruct((2 * half, emb.shape[1]), jnp.bfloat16),
        in_specs=[
            pl.BlockSpec(memory_space=pltpu.SMEM),
            pl.BlockSpec(memory_space=pltpu.VMEM),
        ],
        out_specs=pl.BlockSpec(memory_space=pltpu.VMEM),
        compiler_params=pltpu.CompilerParams(vmem_limit_bytes=20 * 2**20),
    )(source, emb)


def exchange(owners, half, kernel_id, pairs, emb, weight):
    steps = owners // PLANE + 1
    slab = jax.ShapeDtypeStruct((owners, half, 2 * HEAD), jnp.bfloat16)
    return pl.pallas_call(
        functools.partial(exchange_kernel, owners),
        out_shape=(jax.ShapeDtypeStruct((owners,) + pairs.shape, jnp.int32), slab, slab),
        in_specs=[pl.BlockSpec(memory_space=pltpu.VMEM)] * 3,
        out_specs=(pl.BlockSpec(memory_space=pl.ANY),) * 3,
        scratch_shapes=[
            pltpu.VMEM((steps, PLANE, half, 2 * HEAD), jnp.bfloat16),
            pltpu.SemaphoreType.DMA((steps, PLANE)),
            pltpu.SemaphoreType.DMA((owners,)),
            pltpu.SemaphoreType.DMA((owners,)),
            pltpu.SemaphoreType.DMA((owners // PLANE, PLANE)),
            pltpu.SemaphoreType.DMA((3,)),
            pltpu.SemaphoreType.DMA((owners,)),
            pltpu.SemaphoreType.DMA((owners,)),
        ],
        compiler_params=pltpu.CompilerParams(
            collective_id=kernel_id, has_side_effects=True, vmem_limit_bytes=40 * 2**20
        ),
        cost_estimate=pl.CostEstimate(
            flops=4 * half * weight.size, bytes_accessed=40 * 2**20, transcendentals=0
        ),
    )(pairs, emb, weight)


def return_kernel(owners, mass_ref, back_ref, send_sem, recv_sem, local_sem):
    me = lax.axis_index("own")
    barrier = pltpu.get_barrier_semaphore()
    for k in range(1, owners):
        pl.semaphore_signal(
            barrier, inc=1, device_id={"own": (me + k) % owners}, device_id_type=pl.DeviceIdType.MESH
        )
    pl.semaphore_wait(barrier, owners - 1)

    def copy_to(k):
        target = (me + k) % owners
        return pltpu.make_async_remote_copy(
            src_ref=mass_ref.at[target],
            dst_ref=back_ref.at[me],
            send_sem=send_sem.at[k],
            recv_sem=recv_sem.at[me],
            device_id={"own": target},
            device_id_type=pl.DeviceIdType.MESH,
        )

    def copy_from(k):
        source = (me + k) % owners
        return pltpu.make_async_remote_copy(
            src_ref=mass_ref.at[source],
            dst_ref=back_ref.at[source],
            send_sem=send_sem.at[k],
            recv_sem=recv_sem.at[source],
            device_id={"own": source},
            device_id_type=pl.DeviceIdType.MESH,
        )

    sent = [copy_to(k) for k in range(1, owners)]
    for copy in sent:
        copy.start()
    here = pltpu.make_async_copy(mass_ref.at[me], back_ref.at[me], local_sem)
    here.start()
    for k in range(1, owners):
        copy_from(k).wait_recv()
    here.wait()
    for copy in sent:
        copy.wait_send()


def give_back(owners, kernel_id, mass):
    return pl.pallas_call(
        functools.partial(return_kernel, owners),
        out_shape=jax.ShapeDtypeStruct(mass.shape, mass.dtype),
        in_specs=[pl.BlockSpec(memory_space=pltpu.VMEM)],
        out_specs=pl.BlockSpec(memory_space=pltpu.VMEM),
        scratch_shapes=[
            pltpu.SemaphoreType.DMA((owners,)),
            pltpu.SemaphoreType.DMA((owners,)),
            pltpu.SemaphoreType.DMA,
        ],
        compiler_params=pltpu.CompilerParams(collective_id=kernel_id, has_side_effects=True),
    )(mass)


def pairs_kernel(
    per_device, pair_ref, slot_ref, len_ref, start_ref, part_ref, main_ref, extra_ref, out_ref, table
):
    owners, half, lanes = main_ref.shape
    residues = out_ref.shape[3]
    pair_count = pair_ref.shape[0] // 2
    share = pair_count // PLANE
    scale = math.log2(math.e) / math.sqrt(HEAD)

    out_ref[...] = jnp.zeros_like(out_ref)
    lane = lax.broadcasted_iota(jnp.int32, (residues, lanes), 1)
    position = lax.broadcasted_iota(jnp.int32, (residues, lanes), 0)
    low = lane < HEAD

    table[owners * 2 * half :, :] = jnp.zeros((residues, lanes), jnp.bfloat16)
    strip = half // 2
    low_strip = lax.broadcasted_iota(jnp.int32, (strip, lanes), 1) < HEAD

    @pl.loop(0, owners)
    def _(source):
        for p in range(half // strip):
            m = main_ref[source, p * strip : (p + 1) * strip, :].astype(jnp.float32)
            e = extra_ref[source, p * strip : (p + 1) * strip, :].astype(jnp.float32)
            first = pl.multiple_of(source * 2 * half + p * strip, GRANULE)
            second = pl.multiple_of(source * 2 * half + half + p * strip, GRANULE)
            one = jnp.where(low_strip, m, pltpu.roll(e, HEAD, 1))
            two = jnp.where(low_strip, pltpu.roll(m, HEAD, 1), e)
            table[pl.ds(first, strip), :] = one.astype(jnp.bfloat16)
            table[pl.ds(second, strip), :] = two.astype(jnp.bfloat16)

    small = lax.broadcasted_iota(jnp.int32, (16, lanes), 1)
    top = lax.broadcasted_iota(jnp.int32, (16, lanes), 0) == 0

    def facts(k):
        a, b = pair_ref[2 * k], pair_ref[2 * k + 1]
        return slot_ref[a], slot_ref[b], len_ref[a], len_ref[b]

    def rows(row):
        start = row // per_device * (2 * half) + start_ref[row] * GRANULE
        return table[pl.ds(pl.multiple_of(start, GRANULE), residues), :]

    def pick(row, extra):
        left = rows(row)
        keep = low if not extra else jnp.logical_not(low)
        return jnp.where(keep, left, jnp.zeros_like(left))

    def inner(x, y):
        return lax.dot_general(x, y, (((1,), (1,)), ((), ())), preferred_element_type=jnp.float32)

    def outer(x, y):
        return lax.dot_general(x, y, (((1,), (0,)), ((), ())), preferred_element_type=jnp.float32)

    def two_parts(x):
        high = x.astype(jnp.bfloat16).astype(jnp.float32)
        return jnp.where(top, high, x - high).astype(jnp.bfloat16)

    def ratio_of(number, n_a, n_b):
        fa = jnp.full((1, lanes), n_a, jnp.int32).astype(jnp.float32)
        fb = jnp.full((1, lanes), n_b, jnp.int32).astype(jnp.float32)
        return fa / fb, fb / fa

    def add(row, kind, value):
        owner, place = row // per_device, row % per_device
        out_ref[owner, kind, pl.ds(place, 1), :] += value

    def fast(extra, ks, bad):
        known = [facts(k) for k in ks]
        scores = [inner(pick(ra, extra), rows(rb)) for ra, rb, _, _ in known]
        weights = [jnp.exp2(s * scale).astype(jnp.bfloat16) for s in scores]
        live_i = [small < na for _, _, na, _ in known]
        live_j = [small < nb for _, _, _, nb in known]
        row_tot = [
            inner(jnp.where(j, 1.0, 0.0).astype(jnp.bfloat16), w) for j, w in zip(live_j, weights)
        ]
        col_tot = [
            outer(jnp.where(i, 1.0, 0.0).astype(jnp.bfloat16), w) for i, w in zip(live_i, weights)
        ]
        for i, j, r, c in zip(live_i, live_j, row_tot, col_tot):
            fine_r = (r > LOW) & (r < HIGH)
            fine_c = (c > LOW) & (c < HIGH)
            bad = bad + jnp.where(i, jnp.where(fine_r, 0.0, 1.0), 0.0)
            bad = bad + jnp.where(j, jnp.where(fine_c, 0.0, 1.0), 0.0)
        r_inv = [two_parts(jnp.where(i, 1.0 / r, 0.0)) for i, r in zip(live_i, row_tot)]
        c_inv = [two_parts(jnp.where(j, 1.0 / c, 0.0)) for j, c in zip(live_j, col_tot)]
        to_b = [outer(r, w) for r, w in zip(r_inv, weights)]
        to_a = [inner(c, w) for c, w in zip(c_inv, weights)]
        for (ra, rb, na, nb), i, j, a, b in zip(known, live_i, live_j, to_a, to_b):
            a_over_b, b_over_a = ratio_of(None, na, nb)
            add(ra, int(extra), jnp.where(i[:1], (a[0:1] + a[1:2]) * a_over_b, 0.0))
            add(rb, int(extra), jnp.where(j[:1], (b[0:1] + b[1:2]) * b_over_a, 0.0))
        return bad

    def mass(left, right, n_left, n_right):
        live = (position < n_left) & (lane < n_right)
        masked = jnp.where(live, inner(left, right) * scale, -1e30)
        top_row = jnp.max(masked, axis=1, keepdims=True)
        weight = jnp.where(live, jnp.exp2(masked - top_row), 0.0)
        total = jnp.sum(weight, axis=1, keepdims=True)
        total = total + jnp.where(position[:, :1] < n_left, 0.0, 1.0)
        return jnp.sum(weight / total, axis=0, keepdims=True)

    def safe(extra, k):
        ra, rb, na, nb = facts(k)
        left, right = pick(ra, extra), pick(rb, extra)
        a_over_b, b_over_a = ratio_of(None, na, nb)
        add(ra, int(extra), mass(right, left, nb, na) * a_over_b)
        add(rb, int(extra), mass(left, right, na, nb) * b_over_a)

    start = part_ref[0] * share
    bad = jnp.zeros((16, lanes), jnp.float32)
    bad = lax.fori_loop(
        0,
        pair_count // UNROLL,
        lambda t, bad: fast(False, [t * UNROLL + u for u in range(UNROLL)], bad),
        bad,
    )
    bad = lax.fori_loop(
        0,
        share // UNROLL,
        lambda t, bad: fast(True, [start + t * UNROLL + u for u in range(UNROLL)], bad),
        bad,
    )

    @pl.when(jnp.max(bad) > 0.0)
    def _():
        out_ref[...] = jnp.zeros_like(out_ref)

        @pl.loop(0, pair_count)
        def _(k):
            safe(False, k)

        @pl.loop(0, share)
        def _(k):
            safe(True, start + k)


def pair_sums(per_device, residues, pairs, slot_of, lengths, starts, part, main, extra):
    owners, half, lanes = main.shape
    smem = pl.BlockSpec(memory_space=pltpu.SMEM)
    vmem = pl.BlockSpec(memory_space=pltpu.VMEM)
    return pl.pallas_call(
        functools.partial(pairs_kernel, per_device),
        out_shape=jax.ShapeDtypeStruct((owners, 2, per_device, residues), jnp.float32),
        in_specs=[smem] * 5 + [vmem] * 2,
        out_specs=vmem,
        scratch_shapes=[
            pltpu.VMEM((owners * 2 * half + residues, lanes), jnp.bfloat16),
        ],
        compiler_params=pltpu.CompilerParams(vmem_limit_bytes=44 * 2**20),
    )(pairs, slot_of, lengths, starts, part, main, extra)


def local_split(embeddings, lengths, proj_weight, slot_of, pairs):
    per_device, residues, channels = embeddings.shape
    owners = lax.axis_size("own")
    own = lax.axis_index("own")
    full = per_device * residues // 2
    ladder = [full * step // LADDER[-1] for step in LADDER]
    row_ids = jnp.arange(owners * per_device, dtype=jnp.int32)
    row_len = jnp.sum(jnp.where(slot_of[None, :] == row_ids[:, None], lengths[None, :], 0), axis=1)
    count = ((row_len + GRANULE - 1) // GRANULE).reshape(owners, per_device)
    place = jnp.arange(per_device, dtype=jnp.int32)
    starts = jnp.sum(jnp.where(place[None, None, :] < place[None, :, None], count[:, None, :], 0), axis=2)
    need = jnp.max(jnp.sum(count, axis=1))
    groups = lax.axis_size("groups")
    most = need.reshape(1)
    for k in range(1, groups):
        ring = [(g, (g + k) % groups) for g in range(groups)]
        most = jnp.maximum(most, lax.ppermute(need.reshape(1), "groups", ring))
    need = most[0]
    numbers = pairs.size
    padded = -(-numbers // 1024) * 1024
    pair_tile = jnp.pad(pairs.reshape(-1), (0, padded - numbers)).reshape(-1, 128)
    my_start = lax.dynamic_index_in_dim(starts, own, 0, False)
    my_count = lax.dynamic_index_in_dim(count, own, 0, False)
    granules = jnp.arange(2 * full // GRANULE, dtype=jnp.int32)
    offset = granules[:, None] - my_start[None, :]
    source = jnp.sum(
        jnp.where(
            (offset >= 0) & (offset < my_count[None, :]),
            offset + place[None, :] * (residues // GRANULE),
            0,
        ),
        axis=1,
    )
    part = (own % PLANE).reshape(1)
    rows = embeddings.reshape(per_device * residues, channels)

    def branch(kernel_id, half):
        def run():
            known, main, extra = exchange(owners, half, kernel_id, pair_tile, pack(half, source, rows), proj_weight)
            all_pairs = known.reshape(owners, -1)[:, :numbers].reshape(-1)
            return pair_sums(
                per_device, residues, all_pairs, slot_of, lengths, starts.reshape(-1), part, main, extra
            )

        return run

    choice = sum((need * GRANULE > 2 * half).astype(jnp.int32) for half in ladder[:-1])
    mass = lax.switch(choice, [branch(k, half) for k, half in enumerate(ladder)])
    back = give_back(owners, len(ladder), mass)
    first = back[:, 0]
    rest = back[:, 1].reshape(owners // PLANE, PLANE, per_device, residues).sum(axis=1)
    return jnp.concatenate([first, rest], axis=0).transpose(1, 0, 2)


def split_by_heads(mesh):
    owners = mesh.shape["own"]
    return owners % PLANE == 0 and HEADS == owners + owners // PLANE and owners // PLANE == PLANE


def solution(mesh):
    placed = (
        P(("groups", "own"), None, None),
        P("groups"),
        P(),
        P("groups"),
        P(("groups", "own"), None),
    )
    return jax.shard_map(
        local_split if split_by_heads(mesh) else local_any,
        mesh=mesh,
        in_specs=placed,
        out_specs=P(("groups", "own"), None, None),
        check_vma=False,
    )
```

```python
import functools
import math

import jax
import jax.numpy as jnp
from jax import lax
from jax.experimental import pallas as pl
from jax.experimental.pallas import tpu as pltpu
from jax.sharding import PartitionSpec as P

HEADS = 20
CAP = 2
HEAD = 64
PLANE = 4
UNROLL = 24
LOW, HIGH = 2.0**-60, 2.0**60
GRANULE = 16
LADDER = (22, 23, 24, 26, 32)

block_pairs = 8


def pair_mass(query, partner, len_query, len_partner):
    batch, residues, channels = query.shape
    head_size = channels // HEADS
    left = query.reshape(batch, residues, HEADS, head_size)
    right = partner.reshape(batch, residues, HEADS, head_size)
    scores = jnp.einsum(
        "bihe,bjhe->bhij", left, right, preferred_element_type=jnp.float32
    ) / math.sqrt(head_size)
    positions = jnp.arange(residues, dtype=jnp.int32)
    rows_live = positions[None, :] < len_query[:, None]
    cols_live = positions[None, :] < len_partner[:, None]
    live = rows_live[:, None, :, None] & cols_live[:, None, None, :]
    masked = jnp.where(live, scores, -1e30)
    row_top = jnp.max(masked, axis=3, keepdims=True)
    row_exp = jnp.where(live, jnp.exp(masked - row_top), 0.0)
    row_total = (
        jnp.sum(row_exp, axis=3, keepdims=True) + jnp.where(rows_live, 0.0, 1.0)[:, None, :, None]
    )
    to_partner = jnp.sum(row_exp / row_total, axis=2)
    col_top = jnp.max(masked, axis=2, keepdims=True)
    col_exp = jnp.where(live, jnp.exp(masked - col_top), 0.0)
    col_total = (
        jnp.sum(col_exp, axis=2, keepdims=True) + jnp.where(cols_live, 0.0, 1.0)[:, None, None, :]
    )
    to_query = jnp.sum(col_exp / col_total, axis=3)
    ratio = len_partner.astype(jnp.float32) / len_query.astype(jnp.float32)
    return (to_query / ratio[:, None, None], to_partner * ratio[:, None, None])


def local_any(embeddings, lengths, proj_weight, slot_of, pairs):
    per_device, residues, channels = embeddings.shape
    owners = lax.axis_size("own")
    own_index = lax.axis_index("own")
    pair_count = pairs.shape[0]
    row_first = jnp.take(slot_of, pairs[:, 0])
    row_second = jnp.take(slot_of, pairs[:, 1])
    len_first = jnp.take(lengths, pairs[:, 0])
    len_second = jnp.take(lengths, pairs[:, 1])
    local_first = row_first - own_index * per_device
    holder_second = row_second // per_device
    local_second = row_second % per_device
    order_ids = jnp.arange(pair_count, dtype=jnp.int32)
    earlier = (holder_second[:, None] == holder_second[None, :]) & (
        order_ids[None, :] < order_ids[:, None]
    )
    rank = jnp.sum(earlier.astype(jnp.int32), axis=1)
    placed = holder_second * CAP + rank
    slot_count = owners * CAP
    slot_ids = jnp.arange(slot_count, dtype=jnp.int32)
    wanted = (
        jnp.sum(
            jnp.where(placed[:, None] == slot_ids[None, :], local_second[:, None] + 1, 0), axis=0
        )
        - 1
    )
    asked = lax.all_to_all(
        wanted.reshape(owners, CAP), "own", split_axis=0, concat_axis=0, tiled=True
    ).reshape(slot_count)
    features = jnp.dot(
        embeddings.reshape(per_device * residues, channels),
        proj_weight,
        preferred_element_type=jnp.float32,
    )
    features = features.astype(jnp.bfloat16).reshape(per_device, residues, channels)
    outgoing = jnp.take(features, jnp.maximum(asked, 0), axis=0)
    arrived = lax.all_to_all(
        outgoing.reshape(owners, CAP, residues, channels),
        "own",
        split_axis=0,
        concat_axis=0,
        tiled=True,
    )
    arrived = arrived.reshape(slot_count, residues, channels)
    device_rows = jnp.arange(per_device, dtype=jnp.int32)

    def step(carry, item):
        own_total, slot_total = carry
        first_local, slot_place, first_len, second_len = item
        query = jnp.take(features, first_local, axis=0)
        partner = jnp.take(arrived, slot_place, axis=0)
        to_query, to_partner = pair_mass(query, partner, first_len, second_len)
        own_hits = (first_local[:, None] == device_rows[None, :]).astype(jnp.float32)
        slot_hits = (slot_place[:, None] == slot_ids[None, :]).astype(jnp.float32)
        own_total = own_total + jnp.einsum(
            "bp,bhl->phl", own_hits, to_query, precision=lax.Precision.HIGHEST
        )
        slot_total = slot_total + jnp.einsum(
            "bs,bhl->shl", slot_hits, to_partner, precision=lax.Precision.HIGHEST
        )
        return ((own_total, slot_total), None)

    blocks = pair_count // block_pairs
    items = (
        local_first.reshape(blocks, block_pairs),
        placed.reshape(blocks, block_pairs),
        len_first.reshape(blocks, block_pairs),
        len_second.reshape(blocks, block_pairs),
    )
    start = (
        jnp.zeros((per_device, HEADS, residues), jnp.float32),
        jnp.zeros((slot_count, HEADS, residues), jnp.float32),
    )
    (own_total, slot_total), _ = lax.scan(step, start, items)
    slot_rows = slot_ids // CAP * per_device + wanted
    all_rows = jnp.arange(owners * per_device, dtype=jnp.int32)
    row_hits = ((slot_rows[:, None] == all_rows[None, :]) & (wanted >= 0)[:, None]).astype(
        jnp.float32
    )
    spread = jnp.einsum("sr,shl->rhl", row_hits, slot_total, precision=lax.Precision.HIGHEST)
    return own_total + lax.psum_scatter(spread, "own", scatter_dimension=0, tiled=True)


def exchange_kernel(
    owners,
    pair_ref,
    packed,
    w_ref,
    known_ref,
    main_ref,
    extra_ref,
    stage,
    send_sem,
    recv_main,
    recv_extra,
    fwd_sem,
    local_sem,
    pair_sem,
    recv_pair,
):
    me = lax.axis_index("own")
    planes = owners // PLANE
    z, part = me // PLANE, me % PLANE
    half = packed.shape[0] // 2
    tile = half // 2
    wide = PLANE * HEAD

    barrier = pltpu.get_barrier_semaphore()
    for k in range(1, owners):
        pl.semaphore_signal(
            barrier, inc=1, device_id={"own": (me + k) % owners}, device_id_type=pl.DeviceIdType.MESH
        )
    pl.semaphore_wait(barrier, owners - 1)

    low = lax.broadcasted_iota(jnp.int32, (tile, 2 * HEAD), 1) < HEAD

    def project(step, column):
        @pl.loop(0, half // tile)
        def _(t):
            row = pl.multiple_of(t * tile, tile)
            weight = w_ref[:, pl.ds(column, wide)]
            top = jnp.dot(packed[pl.ds(row, tile), :], weight, preferred_element_type=jnp.float32)
            bottom = jnp.dot(
                packed[pl.ds(half + row, tile), :], weight, preferred_element_type=jnp.float32
            )
            for g in range(wide // (2 * HEAD)):
                a = top[:, 2 * HEAD * g : 2 * HEAD * (g + 1)]
                b = bottom[:, 2 * HEAD * g : 2 * HEAD * (g + 1)]
                even = jnp.where(low, a, pltpu.roll(b, HEAD, 1))
                odd = jnp.where(low, pltpu.roll(a, HEAD, 1), b)
                stage[step, 2 * g, pl.ds(row, tile), :] = even.astype(jnp.bfloat16)
                stage[step, 2 * g + 1, pl.ds(row, tile), :] = odd.astype(jnp.bfloat16)

    def remote(src, dst, send, recv, target):
        return pltpu.make_async_remote_copy(
            src_ref=src,
            dst_ref=dst,
            send_sem=send,
            recv_sem=recv,
            device_id={"own": target},
            device_id_type=pl.DeviceIdType.MESH,
        )

    sent = []
    locals_ = []
    for k in range(1, owners):
        copy = remote(
            pair_ref, known_ref.at[me], pair_sem.at[k], recv_pair.at[me], (me + k) % owners
        )
        copy.start()
        sent.append(copy)
    copy = pltpu.make_async_copy(pair_ref, known_ref.at[me], local_sem.at[2])
    copy.start()
    locals_.append(copy)
    project(0, owners * HEAD)
    for k in (2, 1, 3):
        q = (z + k) % planes
        copy = remote(
            stage.at[0, q], extra_ref.at[me], send_sem.at[0, k], recv_extra.at[me], q * PLANE + part
        )
        copy.start()
        sent.append(copy)
    copy = pltpu.make_async_copy(stage.at[0, z], extra_ref.at[me], local_sem.at[0])
    copy.start()
    locals_.append(copy)
    for j in range(1, PLANE):
        peer = z * PLANE + (part + j) % PLANE
        copy = remote(
            stage.at[0, z], extra_ref.at[me], fwd_sem.at[0, j], recv_extra.at[me], peer
        )
        copy.start()
        sent.append(copy)
    for step, k in enumerate((2, 1, 3, 0), 1):
        plane = (z + k) % planes
        project(step, pl.multiple_of(plane * wide, wide))
        for j in range(PLANE):
            other = (part + j) % PLANE
            if k == 0 and j == 0:
                copy = pltpu.make_async_copy(stage.at[step, other], main_ref.at[me], local_sem.at[1])
                copy.start()
                locals_.append(copy)
                continue
            copy = remote(
                stage.at[step, other],
                main_ref.at[me],
                send_sem.at[step, j],
                recv_main.at[me],
                plane * PLANE + other,
            )
            copy.start()
            sent.append(copy)

    def arrived(ref, sem, source):
        remote(ref.at[source], ref.at[source], fwd_sem.at[0, 0], sem.at[source], (me + 1) % owners).wait_recv()

    for k in (1, 3, 2):
        source = (z + k) % planes * PLANE + part
        arrived(extra_ref, recv_extra, source)
        for j in range(1, PLANE):
            peer = z * PLANE + (part + j) % PLANE
            copy = remote(
                extra_ref.at[source], extra_ref.at[source], fwd_sem.at[k, j], recv_extra.at[source], peer
            )
            copy.start()
            sent.append(copy)
    for k in range(planes):
        for j in range(1, PLANE):
            arrived(extra_ref, recv_extra, (z + k) % planes * PLANE + (part + j) % PLANE)
    for k in range(1, owners):
        arrived(known_ref, recv_pair, (me + k) % owners)
        arrived(main_ref, recv_main, (me + k) % owners)
    for copy in locals_:
        copy.wait()
    for copy in sent:
        copy.wait_send()


def pack_kernel(source_ref, emb_ref, packed):
    @pl.loop(0, packed.shape[0] // GRANULE, unroll=4)
    def _(g):
        start = pl.multiple_of(source_ref[g] * GRANULE, GRANULE)
        here = pl.multiple_of(g * GRANULE, GRANULE)
        packed[pl.ds(here, GRANULE), :] = emb_ref[pl.ds(start, GRANULE), :]


def pack(half, source, emb):
    return pl.pallas_call(
        pack_kernel,
        out_shape=jax.ShapeDtypeStruct((2 * half, emb.shape[1]), jnp.bfloat16),
        in_specs=[
            pl.BlockSpec(memory_space=pltpu.SMEM),
            pl.BlockSpec(memory_space=pltpu.VMEM),
        ],
        out_specs=pl.BlockSpec(memory_space=pltpu.VMEM),
        compiler_params=pltpu.CompilerParams(vmem_limit_bytes=20 * 2**20),
    )(source, emb)


def exchange(owners, half, kernel_id, pairs, emb, weight):
    steps = owners // PLANE + 1
    slab = jax.ShapeDtypeStruct((owners, half, 2 * HEAD), jnp.bfloat16)
    return pl.pallas_call(
        functools.partial(exchange_kernel, owners),
        out_shape=(jax.ShapeDtypeStruct((owners,) + pairs.shape, jnp.int32), slab, slab),
        in_specs=[pl.BlockSpec(memory_space=pltpu.VMEM)] * 3,
        out_specs=(pl.BlockSpec(memory_space=pl.ANY),) * 3,
        scratch_shapes=[
            pltpu.VMEM((steps, PLANE, half, 2 * HEAD), jnp.bfloat16),
            pltpu.SemaphoreType.DMA((steps, PLANE)),
            pltpu.SemaphoreType.DMA((owners,)),
            pltpu.SemaphoreType.DMA((owners,)),
            pltpu.SemaphoreType.DMA((owners // PLANE, PLANE)),
            pltpu.SemaphoreType.DMA((3,)),
            pltpu.SemaphoreType.DMA((owners,)),
            pltpu.SemaphoreType.DMA((owners,)),
        ],
        compiler_params=pltpu.CompilerParams(
            collective_id=kernel_id, has_side_effects=True, vmem_limit_bytes=40 * 2**20
        ),
        cost_estimate=pl.CostEstimate(
            flops=4 * half * weight.size, bytes_accessed=40 * 2**20, transcendentals=0
        ),
    )(pairs, emb, weight)


def return_kernel(owners, mass_ref, back_ref, send_sem, recv_sem, local_sem):
    me = lax.axis_index("own")
    barrier = pltpu.get_barrier_semaphore()
    for k in range(1, owners):
        pl.semaphore_signal(
            barrier, inc=1, device_id={"own": (me + k) % owners}, device_id_type=pl.DeviceIdType.MESH
        )
    pl.semaphore_wait(barrier, owners - 1)

    def copy_to(k):
        target = (me + k) % owners
        return pltpu.make_async_remote_copy(
            src_ref=mass_ref.at[target],
            dst_ref=back_ref.at[me],
            send_sem=send_sem.at[k],
            recv_sem=recv_sem.at[me],
            device_id={"own": target},
            device_id_type=pl.DeviceIdType.MESH,
        )

    def copy_from(k):
        source = (me + k) % owners
        return pltpu.make_async_remote_copy(
            src_ref=mass_ref.at[source],
            dst_ref=back_ref.at[source],
            send_sem=send_sem.at[k],
            recv_sem=recv_sem.at[source],
            device_id={"own": source},
            device_id_type=pl.DeviceIdType.MESH,
        )

    sent = [copy_to(k) for k in range(1, owners)]
    for copy in sent:
        copy.start()
    here = pltpu.make_async_copy(mass_ref.at[me], back_ref.at[me], local_sem)
    here.start()
    for k in range(1, owners):
        copy_from(k).wait_recv()
    here.wait()
    for copy in sent:
        copy.wait_send()


def give_back(owners, kernel_id, mass):
    return pl.pallas_call(
        functools.partial(return_kernel, owners),
        out_shape=jax.ShapeDtypeStruct(mass.shape, mass.dtype),
        in_specs=[pl.BlockSpec(memory_space=pltpu.VMEM)],
        out_specs=pl.BlockSpec(memory_space=pltpu.VMEM),
        scratch_shapes=[
            pltpu.SemaphoreType.DMA((owners,)),
            pltpu.SemaphoreType.DMA((owners,)),
            pltpu.SemaphoreType.DMA,
        ],
        compiler_params=pltpu.CompilerParams(collective_id=kernel_id, has_side_effects=True),
    )(mass)


def pairs_kernel(
    per_device, pair_ref, slot_ref, len_ref, start_ref, part_ref, main_ref, extra_ref, out_ref, table
):
    owners, half, lanes = main_ref.shape
    residues = out_ref.shape[3]
    pair_count = pair_ref.shape[0] // 2
    share = pair_count // PLANE
    scale = math.log2(math.e) / math.sqrt(HEAD)

    out_ref[...] = jnp.zeros_like(out_ref)
    lane = lax.broadcasted_iota(jnp.int32, (residues, lanes), 1)
    position = lax.broadcasted_iota(jnp.int32, (residues, lanes), 0)
    low = lane < HEAD

    table[owners * 2 * half :, :] = jnp.zeros((residues, lanes), jnp.bfloat16)
    strip = half // 2
    low_strip = lax.broadcasted_iota(jnp.int32, (strip, lanes), 1) < HEAD

    @pl.loop(0, owners)
    def _(source):
        for p in range(half // strip):
            m = main_ref[source, p * strip : (p + 1) * strip, :].astype(jnp.float32)
            e = extra_ref[source, p * strip : (p + 1) * strip, :].astype(jnp.float32)
            first = pl.multiple_of(source * 2 * half + p * strip, GRANULE)
            second = pl.multiple_of(source * 2 * half + half + p * strip, GRANULE)
            one = jnp.where(low_strip, m, pltpu.roll(e, HEAD, 1))
            two = jnp.where(low_strip, pltpu.roll(m, HEAD, 1), e)
            table[pl.ds(first, strip), :] = one.astype(jnp.bfloat16)
            table[pl.ds(second, strip), :] = two.astype(jnp.bfloat16)

    small = lax.broadcasted_iota(jnp.int32, (16, lanes), 1)
    top = lax.broadcasted_iota(jnp.int32, (16, lanes), 0) == 0

    def facts(k):
        a, b = pair_ref[2 * k], pair_ref[2 * k + 1]
        return slot_ref[a], slot_ref[b], len_ref[a], len_ref[b]

    def rows(row):
        start = row // per_device * (2 * half) + start_ref[row] * GRANULE
        return table[pl.ds(pl.multiple_of(start, GRANULE), residues), :]

    def pick(row, extra):
        left = rows(row)
        keep = low if not extra else jnp.logical_not(low)
        return jnp.where(keep, left, jnp.zeros_like(left))

    def inner(x, y):
        return lax.dot_general(x, y, (((1,), (1,)), ((), ())), preferred_element_type=jnp.float32)

    def outer(x, y):
        return lax.dot_general(x, y, (((1,), (0,)), ((), ())), preferred_element_type=jnp.float32)

    def two_parts(x):
        high = x.astype(jnp.bfloat16).astype(jnp.float32)
        return jnp.where(top, high, x - high).astype(jnp.bfloat16)

    def ratio_of(number, n_a, n_b):
        fa = jnp.full((1, lanes), n_a, jnp.int32).astype(jnp.float32)
        fb = jnp.full((1, lanes), n_b, jnp.int32).astype(jnp.float32)
        return fa / fb, fb / fa

    def add(row, kind, value):
        owner, place = row // per_device, row % per_device
        out_ref[owner, kind, pl.ds(place, 1), :] += value

    def fast(extra, ks, bad):
        known = [facts(k) for k in ks]
        scores = [inner(pick(ra, extra), rows(rb)) for ra, rb, _, _ in known]
        weights = [jnp.exp2(s * scale).astype(jnp.bfloat16) for s in scores]
        live_i = [small < na for _, _, na, _ in known]
        live_j = [small < nb for _, _, _, nb in known]
        row_tot = [
            inner(jnp.where(j, 1.0, 0.0).astype(jnp.bfloat16), w) for j, w in zip(live_j, weights)
        ]
        col_tot = [
            outer(jnp.where(i, 1.0, 0.0).astype(jnp.bfloat16), w) for i, w in zip(live_i, weights)
        ]
        for i, j, r, c in zip(live_i, live_j, row_tot, col_tot):
            fine_r = (r > LOW) & (r < HIGH)
            fine_c = (c > LOW) & (c < HIGH)
            bad = bad + jnp.where(i, jnp.where(fine_r, 0.0, 1.0), 0.0)
            bad = bad + jnp.where(j, jnp.where(fine_c, 0.0, 1.0), 0.0)
        r_inv = [two_parts(jnp.where(i, 1.0 / r, 0.0)) for i, r in zip(live_i, row_tot)]
        c_inv = [two_parts(jnp.where(j, 1.0 / c, 0.0)) for j, c in zip(live_j, col_tot)]
        to_b = [outer(r, w) for r, w in zip(r_inv, weights)]
        to_a = [inner(c, w) for c, w in zip(c_inv, weights)]
        for (ra, rb, na, nb), i, j, a, b in zip(known, live_i, live_j, to_a, to_b):
            a_over_b, b_over_a = ratio_of(None, na, nb)
            add(ra, int(extra), jnp.where(i[:1], (a[0:1] + a[1:2]) * a_over_b, 0.0))
            add(rb, int(extra), jnp.where(j[:1], (b[0:1] + b[1:2]) * b_over_a, 0.0))
        return bad

    def mass(left, right, n_left, n_right):
        live = (position < n_left) & (lane < n_right)
        masked = jnp.where(live, inner(left, right) * scale, -1e30)
        top_row = jnp.max(masked, axis=1, keepdims=True)
        weight = jnp.where(live, jnp.exp2(masked - top_row), 0.0)
        total = jnp.sum(weight, axis=1, keepdims=True)
        total = total + jnp.where(position[:, :1] < n_left, 0.0, 1.0)
        return jnp.sum(weight / total, axis=0, keepdims=True)

    def safe(extra, k):
        ra, rb, na, nb = facts(k)
        left, right = pick(ra, extra), pick(rb, extra)
        a_over_b, b_over_a = ratio_of(None, na, nb)
        add(ra, int(extra), mass(right, left, nb, na) * a_over_b)
        add(rb, int(extra), mass(left, right, na, nb) * b_over_a)

    start = part_ref[0] * share
    bad = jnp.zeros((16, lanes), jnp.float32)
    bad = lax.fori_loop(
        0,
        pair_count // UNROLL,
        lambda t, bad: fast(False, [t * UNROLL + u for u in range(UNROLL)], bad),
        bad,
    )
    bad = lax.fori_loop(
        0,
        share // UNROLL,
        lambda t, bad: fast(True, [start + t * UNROLL + u for u in range(UNROLL)], bad),
        bad,
    )

    @pl.when(jnp.max(bad) > 0.0)
    def _():
        out_ref[...] = jnp.zeros_like(out_ref)

        @pl.loop(0, pair_count)
        def _(k):
            safe(False, k)

        @pl.loop(0, share)
        def _(k):
            safe(True, start + k)


def pair_sums(per_device, residues, pairs, slot_of, lengths, starts, part, main, extra):
    owners, half, lanes = main.shape
    smem = pl.BlockSpec(memory_space=pltpu.SMEM)
    vmem = pl.BlockSpec(memory_space=pltpu.VMEM)
    return pl.pallas_call(
        functools.partial(pairs_kernel, per_device),
        out_shape=jax.ShapeDtypeStruct((owners, 2, per_device, residues), jnp.float32),
        in_specs=[smem] * 5 + [vmem] * 2,
        out_specs=vmem,
        scratch_shapes=[
            pltpu.VMEM((owners * 2 * half + residues, lanes), jnp.bfloat16),
        ],
        compiler_params=pltpu.CompilerParams(vmem_limit_bytes=44 * 2**20),
    )(pairs, slot_of, lengths, starts, part, main, extra)


def local_split(embeddings, lengths, proj_weight, slot_of, pairs):
    per_device, residues, channels = embeddings.shape
    owners = lax.axis_size("own")
    own = lax.axis_index("own")
    full = per_device * residues // 2
    ladder = [full * step // LADDER[-1] for step in LADDER]
    row_ids = jnp.arange(owners * per_device, dtype=jnp.int32)
    row_len = jnp.sum(jnp.where(slot_of[None, :] == row_ids[:, None], lengths[None, :], 0), axis=1)
    count = ((row_len + GRANULE - 1) // GRANULE).reshape(owners, per_device)
    place = jnp.arange(per_device, dtype=jnp.int32)
    starts = jnp.sum(jnp.where(place[None, None, :] < place[None, :, None], count[:, None, :], 0), axis=2)
    need = jnp.max(jnp.sum(count, axis=1))
    groups = lax.axis_size("groups")
    most = need.reshape(1)
    for k in range(1, groups):
        ring = [(g, (g + k) % groups) for g in range(groups)]
        most = jnp.maximum(most, lax.ppermute(need.reshape(1), "groups", ring))
    need = most[0]
    numbers = pairs.size
    padded = -(-numbers // 1024) * 1024
    pair_tile = jnp.pad(pairs.reshape(-1), (0, padded - numbers)).reshape(-1, 128)
    my_start = lax.dynamic_index_in_dim(starts, own, 0, False)
    my_count = lax.dynamic_index_in_dim(count, own, 0, False)
    granules = jnp.arange(2 * full // GRANULE, dtype=jnp.int32)
    offset = granules[:, None] - my_start[None, :]
    source = jnp.sum(
        jnp.where(
            (offset >= 0) & (offset < my_count[None, :]),
            offset + place[None, :] * (residues // GRANULE),
            0,
        ),
        axis=1,
    )
    part = (own % PLANE).reshape(1)
    rows = embeddings.reshape(per_device * residues, channels)

    def branch(kernel_id, half):
        def run():
            known, main, extra = exchange(owners, half, kernel_id, pair_tile, pack(half, source, rows), proj_weight)
            all_pairs = known.reshape(owners, -1)[:, :numbers].reshape(-1)
            return pair_sums(
                per_device, residues, all_pairs, slot_of, lengths, starts.reshape(-1), part, main, extra
            )

        return run

    choice = sum((need * GRANULE > 2 * half).astype(jnp.int32) for half in ladder[:-1])
    mass = lax.switch(choice, [branch(k, half) for k, half in enumerate(ladder)])
    back = give_back(owners, len(ladder), mass)
    first = back[:, 0]
    rest = back[:, 1].reshape(owners // PLANE, PLANE, per_device, residues).sum(axis=1)
    return jnp.concatenate([first, rest], axis=0).transpose(1, 0, 2)


def split_by_heads(mesh):
    owners = mesh.shape["own"]
    return owners % PLANE == 0 and HEADS == owners + owners // PLANE and owners // PLANE == PLANE


def solution(mesh):
    placed = (
        P(("groups", "own"), None, None),
        P("groups"),
        P(),
        P("groups"),
        P(("groups", "own"), None),
    )
    return jax.shard_map(
        local_split if split_by_heads(mesh) else local_any,
        mesh=mesh,
        in_specs=placed,
        out_specs=P(("groups", "own"), None, None),
        check_vma=False,
    )
```
